128 devices in a mesh: patch: 16 (over z, x), exp: 8 (over y, core).
Axes of the slice: x: 4, y: 4, z: 4, core: 2. Of those that a mesh axis runs over, the one named last changes fastest.
Arguments:
- sky_model: float32 [16, 8, 6, 256, 256], P('patch', 'exp'), may hold values from -6 to 6
- stamp_pixels: bfloat16 [16384, 256, 256], P(('patch', 'exp')), may hold values from -6 to 6
- stamp_patch: int32 [16384, 1], P(('patch', 'exp')), may hold values from 0 to 15; in each aligned block of 128 rows (0 to 127, 128 to 255, ...) at most 12 rows name the same one
- stamp_band: int32 [16384], P(('patch', 'exp')), may hold values from 0 to 5
- psf_taps: bfloat16 [16384, 2, 21], P(('patch', 'exp')), may hold values from 0.019897461 to 0.19921875
- stamp_gain: bfloat16 [16384], P(('patch', 'exp')), may hold values from 0.5 to 2
- stamp_weight: bfloat16 [16384], P(('patch', 'exp')), may hold values from 0.25 to 4
Outputs:
- new_model: float32 [16, 8, 6, 256, 256], P('patch', 'exp')
- step_rms: float32 [], replicated
The draws below stay inside these ranges and needn't reach their ends.
Inputs may be any that keep to these rules, and one draw needn't show every extreme that they name: `stamp_patch`: among the stamps of one device no patch is named by more than 12 stamps, a bound that some block reaches.
All inputs are finite; a program needn't handle non-finite values.
Results may differ from the reference program's by a relative error of at most 0.013.
Values may be sent and summed in bfloat16 or wider, within the bound.
A program may use at most 192 MiB of HBM per device.

```python
import math
import jax
import jax.numpy as jnp
import numpy as np
from jax import lax

BANDS = 6
TS = 256
TAPS = 21
STAMPS_DEV = 128
PATCHES = 16
TILES = 8
STAMPS = 16384
CAP = 12
N_EXP = 8


def place_ends(entries, own_key, least, top_value):
    longest = entries.shape.index(max(entries.shape))
    spots = []
    for shift in (0, 1):
        where = [jax.random.randint(jax.random.fold_in(own_key, axis), (), 0, length) for axis, length in enumerate(entries.shape)]
        where[longest] = (where[longest] + shift) % entries.shape[longest]
        spots.append(tuple(where))
    return entries.at[spots[0]].set(least).at[spots[1]].set(top_value)


def block_levels(stream_key, extent, shards, low, high):
    factor_of, own = 1.0, jax.random.fold_in(stream_key, 6)
    for axis_at, shards_of in shards:
        draws = jnp.exp(jax.random.uniform(jax.random.fold_in(own, axis_at), (shards_of,), jnp.float32, low / len(shards), high / len(shards)))
        factor_of = factor_of * jnp.repeat(draws, extent[axis_at] // shards_of).reshape([-1 if axis == axis_at else 1 for axis in range(len(extent))])
    return factor_of


def deal_out(rng, own, number, rows, count, top, bound, lean):
    sequence = jax.random.permutation(rng, count)
    crowded, usual = shares(count, rows * top, bound, lean, True), shares(count, rows * top, bound, lean, False)
    places = jnp.arange(count)

    def named(lengths, offset_by):
        used = int((lengths > 0).sum())
        fixed = max(1, used // 4)
        passed = fixed + (places - fixed + offset_by * (used - fixed)) % max(1, count - fixed)
        return jnp.zeros((count,), jnp.int32).at[sequence[jnp.where(places < fixed, places, passed)]].set(jnp.asarray(lengths, jnp.int32))

    lengths = jnp.where(number % 4 == 0, named(crowded, number // 4), named(usual, number - number // 4 - 1))
    mixed = jax.random.permutation(jax.random.fold_in(own, 3), count)
    giver, receiver = mixed[0:count // 2 * 2:2], mixed[1:count // 2 * 2:2]
    slack = jnp.minimum(lengths[giver] - 1, bound - lengths[receiver]) // 2
    slack = jnp.where((giver == sequence[0]) | (receiver == sequence[0]) | (lengths[receiver] == 0), 0, jnp.maximum(slack, 0))
    passed = jax.random.randint(jax.random.fold_in(own, 4), (count // 2,), 0, 1 << 20) % (slack + 1)
    lengths = lengths.at[giver].add(-passed).at[receiver].add(passed)
    labels = jnp.searchsorted(jnp.cumsum(lengths), jnp.arange(rows * top), side="right").astype(jnp.int32)
    listing = labels.reshape(top, rows).T
    listing = listing[jax.random.permutation(jax.random.fold_in(own, 1), rows)]
    offset_by = jax.random.randint(jax.random.fold_in(own, 2), (rows, 1), 0, top)
    return jnp.take_along_axis(listing, (jnp.arange(top)[None, :] + offset_by) % top, axis=1)


def shares(amount, total, reach, lean, full):
    portions = [(1 << 20) // math.isqrt(rank ** lean) + 1 for rank in range(1, amount + 1)]
    largest = reach if full else min(reach, max(-(-total // amount), total * portions[0] // sum(portions)))
    least = 1 if total - largest >= amount - 1 else 0
    counts, spare = [largest] + [least] * (amount - 1), total - largest - least * (amount - 1)
    while spare > 0:
        candidates = [i for i in range(1, amount) if counts[i] < largest] or [i for i in range(1, amount) if counts[i] < reach]
        whole, budget = sum([portions[i] for i in candidates]), spare
        for i in candidates:
            addition = min(reach - counts[i], max(1, budget * portions[i] // whole), spare)
            counts[i] = counts[i] + addition
            spare = spare - addition
    return np.array(counts)


def scatter_about(key, shape, spread, limit, split=(), kind=jnp.bfloat16):
    array = jax.random.normal(key, shape, jnp.float32) * spread
    if len(split) > 0:
        array = block_levels(key, shape, split, -0.22, 0.18) * array
    return jnp.clip(array, min=-limit, max=limit).astype(kind)


def setup_inputs(seed: int = 0) -> dict:
    streams_of = jax.random.split(jax.random.key(seed), 8)
    sky_model = scatter_about(streams_of[0], (PATCHES, TILES, BANDS, TS, TS), 1.0, 6.0, ((0, 16), (1, 8)), jnp.float32)
    stamp_pixels = scatter_about(streams_of[1], (STAMPS, TS, TS), 1.0, 6.0, ((0, 128),))
    stamp_patch_keys = jax.random.split(jax.random.fold_in(streams_of[2], 1), STAMPS // STAMPS_DEV)
    stamp_patch_turns = jax.random.permutation(jax.random.fold_in(streams_of[2], 3), STAMPS // STAMPS_DEV)
    stamp_patch = jax.vmap(lambda own, number: deal_out(jax.random.fold_in(streams_of[2], 2), own, number, STAMPS_DEV, PATCHES, 1, CAP, 2))(stamp_patch_keys, stamp_patch_turns).reshape((STAMPS, 1))
    stamp_band = place_ends(jax.random.randint(streams_of[3], (STAMPS,), 0, BANDS), jax.random.fold_in(streams_of[3], 1), 0, BANDS - 1).astype(jnp.int32)
    psf_taps = jnp.clip(jnp.exp(math.log(0.19921875) - 2.3038113 * jax.random.uniform(streams_of[4], (STAMPS, 2, TAPS), jnp.float32) ** block_levels(streams_of[4], (STAMPS, 2, TAPS), ((0, 128),), -0.2, 0.2)), 0.019897461, 0.19921875).astype(jnp.bfloat16)
    stamp_gain = jnp.clip(jnp.exp(math.log(2.0) - 1.3862944 * jax.random.uniform(streams_of[5], (STAMPS,), jnp.float32) ** block_levels(streams_of[5], (STAMPS,), ((0, 128),), -0.2, 0.2)), 0.5, 2.0).astype(jnp.bfloat16)
    stamp_weight = jnp.clip(jnp.exp(math.log(4.0) - 2.7725887 * jax.random.uniform(streams_of[6], (STAMPS,), jnp.float32) ** block_levels(streams_of[6], (STAMPS,), ((0, 128),), -0.2, 0.2)), 0.25, 4.0).astype(jnp.bfloat16)
    return dict(sky_model=sky_model, stamp_pixels=stamp_pixels, stamp_patch=stamp_patch, stamp_band=stamp_band, psf_taps=psf_taps, stamp_gain=stamp_gain, stamp_weight=stamp_weight)


step_rate = 0.2

def widen(value):
    return value.astype(jnp.float32)

def banded_matrices(tap_values, tile_size):
    tap_length = tap_values.shape[-1]
    half_width = (tap_length - 1) // 2
    pixel_index = jnp.arange(tile_size, dtype=jnp.int32)
    offset = pixel_index[None, :] - pixel_index[:, None] + half_width
    tap_table = (offset[None, :, :] == jnp.arange(tap_length, dtype=jnp.int32)[:, None, None]).astype(jnp.float32)
    return jnp.einsum('sk,kij->sij', widen(tap_values), tap_table).astype(jnp.bfloat16)

def stamp_adjoint(tile_sel, pixels, tap_values, gain_rows, weight_rows):
    tile_size = pixels.shape[-1]
    row_kernel = banded_matrices(tap_values[:, 0], tile_size)
    col_kernel = banded_matrices(tap_values[:, 1], tile_size)
    blurred = jnp.einsum('sab,scb->sac', widen(tile_sel), widen(col_kernel)).astype(jnp.bfloat16)
    gain_wide = widen(gain_rows)[:, None, None]
    predicted = gain_wide * jnp.einsum('sab,sbc->sac', widen(row_kernel), widen(blurred))
    residual = (widen(weight_rows)[:, None, None] * (predicted - widen(pixels))).astype(jnp.bfloat16)
    backward = jnp.einsum('sba,sbc->sac', widen(row_kernel), widen(residual)).astype(jnp.bfloat16)
    return gain_wide * jnp.einsum('sab,sbc->sac', widen(backward), widen(col_kernel))

def reference(sky_model, stamp_pixels, stamp_patch, stamp_band, psf_taps, stamp_gain, stamp_weight):
    key_count = PATCHES * TILES * BANDS
    model_half = sky_model.astype(jnp.bfloat16).reshape(key_count, TS, TS)
    device_total = STAMPS // STAMPS_DEV

    def one_device(running, device):
        start = (device * STAMPS_DEV).astype(jnp.int32)
        pixels = lax.dynamic_slice_in_dim(stamp_pixels, start, STAMPS_DEV, 0)
        patch_rows = lax.dynamic_slice_in_dim(stamp_patch[:, 0], start, STAMPS_DEV, 0)
        band_rows = lax.dynamic_slice_in_dim(stamp_band, start, STAMPS_DEV, 0)
        tap_values = lax.dynamic_slice_in_dim(psf_taps, start, STAMPS_DEV, 0)
        gain_rows = lax.dynamic_slice_in_dim(stamp_gain, start, STAMPS_DEV, 0)
        weight_rows = lax.dynamic_slice_in_dim(stamp_weight, start, STAMPS_DEV, 0)
        group = (device % N_EXP).astype(jnp.int32)
        tile_keys = ((patch_rows * TILES + group) * BANDS + band_rows).astype(jnp.int32)
        tile_sel = jnp.take(model_half, tile_keys, axis=0)
        adjoint = stamp_adjoint(tile_sel, pixels, tap_values, gain_rows, weight_rows)
        return (running + jax.ops.segment_sum(adjoint, tile_keys, num_segments=key_count), None)
    result = lax.scan(one_device, jnp.zeros((key_count, TS, TS), jnp.float32), jnp.arange(device_total, dtype=jnp.int32))
    gradient = result[0].reshape(sky_model.shape)
    step_field = step_rate * gradient
    new_model = sky_model - step_field
    step_rms = jnp.sqrt(jnp.mean(step_field * step_field) + 1e-06)
    return (new_model, step_rms)
```

```python
import functools

import jax
import jax.numpy as jnp
from jax import lax
from jax.experimental import pallas as pl
from jax.experimental.pallas import tpu as pltpu
from jax.sharding import PartitionSpec as P

TS = 256
BANDS = 6
HALF = 3
STAMPS = 128
STEP_RATE = 0.2
F32, BF16 = jnp.float32, jnp.bfloat16
MESH = pl.DeviceIdType.MESH

UNITS = [
    (0, 0), (0, 1), (0, -1), (1, 0), (-1, 0),
    (0, 2), (2, 0), (1, 1), (1, -1), (-1, 1), (-1, -1),
    (2, 1), (2, -1), (1, 2), (-1, 2), (2, 2),
]
UNIT = {offset: number for number, offset in enumerate(UNITS)}
GROUPS = [(0, 5), (5, 11), (11, 16)]
LINKS = [(0, 1), (0, -1), (1, 0), (-1, 0)]


def place_on_torus():
    patch = lax.axis_index("patch")
    return patch // 4, lax.rem(patch, 4)


def neighbour(offset):
    z, x = place_on_torus()
    return lax.rem(z + offset[0] + 4, 4) * 4 + lax.rem(x + offset[1] + 4, 4)


def from_offset(value, offset):
    dz, dx = offset
    pairs = [
        (((z + dz) % 4) * 4 + (x + dx) % 4, z * 4 + x) for z in range(4) for x in range(4)
    ]
    return lax.ppermute(value, "patch", pairs)


def gather_units(low, high):
    first = {(0, 0): (low, high)}
    for link in LINKS[:2]:
        first[link] = [from_offset(low, link)]
    for link in LINKS[2:]:
        first[link] = [from_offset(high, link)]
    for link in LINKS[:2]:
        first[link].append(from_offset(high, link))
    for link in LINKS[2:]:
        first[link].insert(0, from_offset(low, link))
    units = dict(first)
    for dz in (1, -1):
        for dx in (1, -1):
            units[dz, dx] = (
                from_offset(first[0, dx][0], (dz, 0)),
                from_offset(first[dz, 0][1], (0, dx)),
            )
    units[0, 2] = (from_offset(first[0, 1][0], (0, 1)), from_offset(first[0, -1][1], (0, -1)))
    units[2, 0] = (from_offset(first[1, 0][0], (1, 0)), from_offset(first[-1, 0][1], (-1, 0)))
    for d in (1, -1):
        units[2, d] = tuple(from_offset(part, (0, d)) for part in units[2, 0])
        units[d, 2] = tuple(from_offset(part, (d, 0)) for part in units[0, 2])
    out = {k: [(v[0], 0, 0), (v[1], HALF, 0)] for k, v in units.items()}
    out[2, 2] = []
    for quarter, link in enumerate(LINKS):
        via = tuple(2 if d == 0 else d for d in link)
        rows = slice(quarter * 64, quarter * 64 + 64)
        part = jnp.concatenate([p[:, rows] for p in units[via]], 0)
        out[2, 2].append((from_offset(part, link), 0, quarter * 64))
    return out


def tap_rows(taps):
    half = taps.shape[-1] // 2

    def ring(v):
        gap = jnp.zeros(v.shape[:-1] + (128 - v.shape[-1],), v.dtype)
        return jnp.concatenate([v[..., half:], gap, v[..., :half]], -1)

    both = jnp.stack([ring(taps), ring(taps[..., ::-1])], 2)
    both = both.reshape(taps.shape[0], 4, 128).astype(F32)
    return jnp.pad(both, ((0, 0), (0, 4), (0, 0)))


def stamp_order(stamp_patch, stamp_band):
    z, x = place_on_torus()
    dz = lax.rem(stamp_patch // 4 - z + 4, 4)
    dx = lax.rem(lax.rem(stamp_patch, 4) - x + 4, 4)
    offset = dz * 4 + dx
    unit = jnp.zeros_like(offset)
    for number, (a, b) in enumerate(UNITS):
        unit = jnp.where(offset == (a % 4) * 4 + b % 4, number, unit)
    group = (unit >= GROUPS[1][0]).astype(jnp.int32) + (unit >= GROUPS[2][0]).astype(jnp.int32)
    base = jnp.where(group == 0, 0, jnp.where(group == 1, GROUPS[1][0], GROUPS[2][0]))
    tile = (unit - base) * BANDS + stamp_band
    number = jnp.arange(STAMPS, dtype=jnp.int32)
    rank = group * STAMPS + number
    spot = jnp.sum((rank[None, :] < rank[:, None]).astype(jnp.int32), 1)
    here = spot[None, :] == jnp.arange(STAMPS + 8, dtype=jnp.int32)[:, None]
    ids = jnp.sum(jnp.where(here, number[None, :], 0), 1)
    tiles = jnp.sum(jnp.where(here, tile[None, :], 0), 1)
    bounds = jnp.sum((group[None, :] < jnp.arange(4, dtype=jnp.int32)[:, None]).astype(jnp.int32), 1)
    return ids, tiles, bounds


def build(row, dst):
    ring = pltpu.roll(jnp.broadcast_to(row, (128, 128)), 0, 1, stride=1, stride_axis=0)
    d = lax.broadcasted_iota(jnp.int32, (128, 128), 1) - lax.broadcasted_iota(
        jnp.int32, (128, 128), 0
    )
    zero = jnp.zeros_like(ring)
    diag = jnp.where(jnp.abs(d) < 64, ring, zero).astype(BF16)
    dst[0:128, 0:128] = diag
    dst[128:256, 128:256] = diag
    dst[112:128, 128:256] = jnp.where(d < -64, ring, zero)[112:].astype(BF16)
    dst[128:144, 0:128] = jnp.where(d > 64, ring, zero)[:16].astype(BF16)


def dot(a, b):
    return jnp.dot(a, b, preferred_element_type=F32)


def stamps_kernel(group, parts, per, ids, tls, bounds, gain, weight, rows, pix, *rest):
    tin = rest[: len(parts)]
    out = rest[len(parts)]
    tiles, acc, outb, pbuf, mats, blur, resi, back, tsem, psem, osem = rest[len(parts) + 1 :]
    first = bounds[group]
    n = bounds[group + 1] - first
    steps = (n + per - 1) // per
    loads = [
        pltpu.make_async_copy(t, tiles.at[s : s + t.shape[0], r : r + t.shape[1]], tsem.at[k])
        for k, (t, (s, r)) in enumerate(zip(tin, parts))
    ]
    for c in loads:
        c.start()

    def fetch(step, slot):
        return [
            pltpu.make_async_copy(
                pix.at[ids[first + step * per + u]], pbuf.at[slot, u], psem.at[slot, u]
            )
            for u in range(per)
        ]

    @pl.when(steps > 0)
    def _():
        for c in fetch(0, 0):
            c.start()

    acc[...] = jnp.zeros_like(acc)
    mats[...] = jnp.zeros_like(mats)
    for c in loads:
        c.wait()

    def body(step, carry):
        slot = lax.rem(step, 2)

        @pl.when(step + 1 < steps)
        def _():
            for c in fetch(step + 1, 1 - slot):
                c.start()

        at = [step * per + u for u in range(per)]
        idx = [ids[first + a] for a in at]
        for u in range(per):
            for m in range(4):
                build(rows[idx[u], m : m + 1, :], mats.at[u, m])
        for c in fetch(step, slot):
            c.wait()
        t = [jnp.where(a < n, tls[first + a], 0) for a in at]
        g = [jnp.where(a < n, gain[i], 0.0) for a, i in zip(at, idx)]
        w = [weight[i] for i in idx]
        for u in range(per):
            blur[u] = dot(tiles[t[u]], mats[u, 3]).astype(BF16)
        for u in range(per):
            predicted = g[u] * dot(mats[u, 0], blur[u])
            resi[u] = (w[u] * (predicted - pbuf[slot, u].astype(F32))).astype(BF16)
        for u in range(per):
            back[u] = dot(mats[u, 1], resi[u]).astype(BF16)
        for u in range(per):
            acc[t[u]] += g[u] * dot(back[u], mats[u, 2])
        return carry

    lax.fori_loop(0, steps, body, 0)

    @pl.loop(0, acc.shape[0])
    def _(k):
        outb[k] = acc[k].astype(BF16)

    c = pltpu.make_async_copy(outb, out, osem)
    c.start()
    c.wait()


def stamps(group, units, order, gain, weight, rows, pix, per=4):
    lo, hi = GROUPS[group]
    parts, arrays = [], []
    for number in range(lo, hi):
        for array, band, row in units[UNITS[number]]:
            parts.append(((number - lo) * BANDS + band, row))
            arrays.append(array)
    n_tiles = (hi - lo) * BANDS
    smem = pl.BlockSpec(memory_space=pltpu.SMEM)
    anys = pl.BlockSpec(memory_space=pl.ANY)
    return pl.pallas_call(
        functools.partial(stamps_kernel, group, parts, per),
        out_shape=jax.ShapeDtypeStruct((n_tiles, TS, TS), BF16),
        in_specs=[smem] * 5 + [pl.BlockSpec(memory_space=pltpu.VMEM), anys] + [anys] * len(parts),
        out_specs=anys,
        scratch_shapes=[
            pltpu.VMEM((n_tiles, TS, TS), BF16),
            pltpu.VMEM((n_tiles, TS, TS), F32),
            pltpu.VMEM((n_tiles, TS, TS), BF16),
            pltpu.VMEM((2, per, TS, TS), BF16),
            pltpu.VMEM((per, 4, TS, TS), BF16),
            pltpu.VMEM((per, TS, TS), BF16),
            pltpu.VMEM((per, TS, TS), BF16),
            pltpu.VMEM((per, TS, TS), BF16),
            pltpu.SemaphoreType.DMA((len(parts),)),
            pltpu.SemaphoreType.DMA((2, per)),
            pltpu.SemaphoreType.DMA,
        ],
        compiler_params=pltpu.CompilerParams(vmem_limit_bytes=48 * 2**20),
        cost_estimate=pl.CostEstimate(
            flops=8 * TS**3 * 43 * 2, bytes_accessed=16 * 2**20, transcendentals=0
        ),
        name=f"stamps{group}",
    )(*order, gain, weight, rows, pix, *arrays)


def add_into(dst, d0, src, s0, count):
    @pl.loop(0, count)
    def _(k):
        dst[d0 + k] = (dst[d0 + k].astype(F32) + src[s0 + k].astype(F32)).astype(BF16)


def reduce_kernel(g0, g1, g2, sky, out, sq, own, quarter, diag, three, two, one,
                  skyb, lsem, ssem, rsem):
    barrier = pltpu.get_barrier_semaphore()
    for link in LINKS:
        pl.semaphore_signal(
            barrier, inc=1, device_id={"patch": neighbour(link)}, device_id_type=MESH
        )
    loads = [
        pltpu.make_async_copy(g, own.at[lo * BANDS : hi * BANDS], lsem.at[k])
        for k, (g, (lo, hi)) in enumerate(zip((g0, g1, g2), GROUPS))
    ]
    loads.append(pltpu.make_async_copy(sky, skyb, lsem.at[3]))
    for k in (2, 1, 0, 3):
        loads[k].start()
    pl.semaphore_wait(barrier, 4)

    def at(offset, half):
        return UNIT[offset] * BANDS + half * HALF

    def send(link, piece, src, dst):
        return pltpu.make_async_remote_copy(
            src_ref=src,
            dst_ref=dst,
            send_sem=ssem.at[link, piece],
            recv_sem=rsem.at[link, piece],
            device_id={"patch": neighbour(LINKS[link])},
            device_id_type=MESH,
        )

    copies, info = [], []
    for k, link in enumerate(LINKS):
        dz, dx = link
        late = 0 if dz + dx > 0 else 1
        early = 1 - late
        along_x = dz == 0
        far = (2, dx) if along_x else (dz, 2)
        straight = (0, 2) if along_x else (2, 0)
        sides = [(s, dx) if along_x else (dz, s) for s in (1, -1)]
        diag_half = 1 if along_x else 0
        row = [send(k, 0, own.at[at((2, 2), 0) : at((2, 2), 0) + BANDS, k * 64 : k * 64 + 64], quarter.at[k])]

        def half(piece, offset, h, dst):
            return send(k, piece, own.at[at(offset, h) : at(offset, h) + HALF], dst)

        row.append(half(1, sides[0], diag_half, diag.at[k, 0:HALF]))
        row.append(half(2, far, 0, three.at[k, 0:HALF]))
        row.append(half(3, far, 1, three.at[k, HALF:BANDS]))
        row.append(half(4, sides[1], diag_half, diag.at[k, HALF:BANDS]))
        row.append(half(5, straight, late, two.at[k]))
        row.append(half(6, link, early, one.at[k, early * HALF : early * HALF + HALF]))
        row.append(half(7, link, late, one.at[k, late * HALF : late * HALF + HALF]))
        copies.append(row)
        info.append((far, straight, sides, diag_half, early, late))

    loads[2].wait()
    for k in range(4):
        copies[k][0].start()
    loads[1].wait()
    for k in range(4):
        copies[k][1].start()
    for k in range(4):
        copies[k][0].wait_recv()
        far = info[k][0]

        @pl.loop(0, BANDS)
        def _(b):
            t = at(far, 0) + b
            r = slice(k * 64, k * 64 + 64)
            own[t, r] = (own[t, r].astype(F32) + quarter[k, b].astype(F32)).astype(BF16)

        copies[k][2].start()
        copies[k][3].start()
        copies[k][4].start()
    for h in range(2):
        for k in range(4):
            copies[k][2 + h].wait_recv()
            target = (2, 0) if LINKS[k][0] == 0 else (0, 2)
            add_into(own, at(target, h), three.at[k], h * HALF, HALF)
        for k in range(4):
            if info[k][5] == h:
                copies[k][5].start()
    loads[0].wait()
    for k in range(4):
        sides, diag_half = info[k][2:4]
        for s in range(2):
            copies[k][1 if s == 0 else 4].wait_recv()
            dz, dx = sides[s]
            target = (dz, 0) if LINKS[k][0] == 0 else (0, dx)
            add_into(own, at(target, diag_half), diag.at[k], s * HALF, HALF)
    for k in range(4):
        copies[k][6].start()
    for k in range(4):
        copies[k][5].wait_recv()
        add_into(own, at(LINKS[k], info[k][5]), two.at[k], 0, HALF)
        copies[k][7].start()
    loads[3].wait()
    for k in range(4):
        copies[k][6].wait_recv()
        copies[k][7].wait_recv()

    def finish(b, total):
        gradient = own[b].astype(F32)
        for k in range(4):
            gradient = gradient + one[k, b].astype(F32)
        step_field = STEP_RATE * gradient
        skyb[b] = skyb[b] - step_field
        squares = (step_field * step_field).reshape(TS // 8, 8, TS).sum(0)
        return total + squares[:, :128] + squares[:, 128:]

    sq[...] = lax.fori_loop(0, BANDS, finish, jnp.zeros((8, 128), F32))
    c = pltpu.make_async_copy(skyb, out, lsem.at[3])
    c.start()
    for k in range(4):
        for c2 in copies[k]:
            c2.wait_send()
    c.wait()


def reduce_tiles(g0, g1, g2, sky):
    anys = pl.BlockSpec(memory_space=pl.ANY)
    return pl.pallas_call(
        reduce_kernel,
        out_shape=(
            jax.ShapeDtypeStruct((BANDS, TS, TS), F32),
            jax.ShapeDtypeStruct((8, 128), F32),
        ),
        in_specs=[anys] * 4,
        out_specs=(anys, pl.BlockSpec(memory_space=pltpu.VMEM)),
        scratch_shapes=[
            pltpu.VMEM((16 * BANDS, TS, TS), BF16),
            pltpu.VMEM((4, BANDS, 64, TS), BF16),
            pltpu.VMEM((4, BANDS, TS, TS), BF16),
            pltpu.VMEM((4, BANDS, TS, TS), BF16),
            pltpu.VMEM((4, HALF, TS, TS), BF16),
            pltpu.VMEM((4, BANDS, TS, TS), BF16),
            pltpu.VMEM((BANDS, TS, TS), F32),
            pltpu.SemaphoreType.DMA((4,)),
            pltpu.SemaphoreType.DMA((4, 8)),
            pltpu.SemaphoreType.DMA((4, 8)),
        ],
        compiler_params=pltpu.CompilerParams(
            collective_id=1, has_side_effects=True, vmem_limit_bytes=48 * 2**20
        ),
        name="reduce_tiles",
    )(g0, g1, g2, sky)


def total_kernel(sq, out, held, sums, ssem, rsem, ssem2, rsem2):
    patch, exp = lax.axis_index("patch"), lax.axis_index("exp")
    barrier = pltpu.get_barrier_semaphore()
    peers = [("patch", lax.rem(patch + k, 16)) for k in range(1, 16)]
    peers += [("exp", lax.rem(exp + k, 8)) for k in range(1, 8)]
    for peer in peers:
        pl.semaphore_signal(barrier, inc=1, device_id=dict([peer]), device_id_type=MESH)
    pl.semaphore_wait(barrier, len(peers))
    held[patch] = sq[...]
    first = [
        pltpu.make_async_remote_copy(
            src_ref=sq, dst_ref=held.at[patch], send_sem=ssem.at[k], recv_sem=rsem.at[k],
            device_id=dict([peer]), device_id_type=MESH,
        )
        for k, peer in enumerate(peers[:15])
    ]
    for c in first:
        c.start()
    for c in first:
        c.wait()
    sums[exp] = jnp.sum(held[...], 0)
    second = [
        pltpu.make_async_remote_copy(
            src_ref=sums.at[exp], dst_ref=sums.at[exp], send_sem=ssem2.at[k], recv_sem=rsem2.at[k],
            device_id=dict([peer]), device_id_type=MESH,
        )
        for k, peer in enumerate(peers[15:])
    ]
    for c in second:
        c.start()
    for c in second:
        c.wait()
    out[...] = jnp.sum(sums[...], 0)


def total_of(sq):
    vmem = pl.BlockSpec(memory_space=pltpu.VMEM)
    return pl.pallas_call(
        total_kernel,
        out_shape=jax.ShapeDtypeStruct((8, 128), F32),
        in_specs=[vmem],
        out_specs=vmem,
        scratch_shapes=[
            pltpu.VMEM((16, 8, 128), F32),
            pltpu.VMEM((8, 8, 128), F32),
            pltpu.SemaphoreType.DMA((15,)),
            pltpu.SemaphoreType.DMA((15,)),
            pltpu.SemaphoreType.DMA((7,)),
            pltpu.SemaphoreType.DMA((7,)),
        ],
        compiler_params=pltpu.CompilerParams(collective_id=2, has_side_effects=True),
        name="total",
    )(sq)


def per_device(
    sky_model, stamp_pixels, stamp_patch, stamp_band, psf_taps, stamp_gain, stamp_weight
):
    sky = sky_model.reshape(BANDS, TS, TS)
    model_half = sky.astype(BF16)
    units = gather_units(model_half[:HALF], model_half[HALF:])
    order = stamp_order(stamp_patch[:, 0], stamp_band)
    rows = tap_rows(psf_taps)
    gain, weight = stamp_gain.astype(F32), stamp_weight.astype(F32)
    sums = [stamps(k, units, order, gain, weight, rows, stamp_pixels) for k in range(3)]
    new_model, squares = reduce_tiles(*sums, sky)
    square_sum = jnp.sum(total_of(squares))
    entry_count = lax.axis_size("patch") * lax.axis_size("exp") * BANDS * TS * TS
    step_rms = jnp.sqrt(square_sum / entry_count + 1e-06)
    return (new_model.reshape(sky_model.shape), step_rms)


def solution(mesh):
    return jax.shard_map(
        per_device,
        mesh=mesh,
        in_specs=(
            P("patch", "exp", None, None, None),
            P(("patch", "exp"), None, None),
            P(("patch", "exp"), None),
            P(("patch", "exp")),
            P(("patch", "exp"), None, None),
            P(("patch", "exp")),
            P(("patch", "exp")),
        ),
        out_specs=(P("patch", "exp", None, None, None), P()),
        check_vma=False,
    )
```

```python
import functools

import jax
import jax.numpy as jnp
from jax import lax
from jax.experimental import pallas as pl
from jax.experimental.pallas import tpu as pltpu
from jax.sharding import PartitionSpec as P

TS = 256
BANDS = 6
HALF = 3
STAMPS = 128
STEP_RATE = 0.2
F32, BF16 = jnp.float32, jnp.bfloat16
MESH = pl.DeviceIdType.MESH

UNITS = [
    (0, 0), (0, 1), (0, -1), (1, 0), (-1, 0),
    (0, 2), (2, 0), (1, 1), (-1, -1),
    (2, 1), (2, -1), (1, 2), (-1, 2), (1, -1), (-1, 1), (2, 2),
]
UNIT = {offset: number for number, offset in enumerate(UNITS)}
TILES = len(UNITS) * BANDS
LINKS = [(0, 1), (0, -1), (1, 0), (-1, 0)]
PER = 4


def place_on_torus():
    patch = lax.axis_index("patch")
    return patch // 4, lax.rem(patch, 4)


def neighbour(offset):
    z, x = place_on_torus()
    return lax.rem(z + offset[0] + 4, 4) * 4 + lax.rem(x + offset[1] + 4, 4)


def tap_rows(taps):
    half = taps.shape[-1] // 2

    def ring(v):
        gap = jnp.zeros(v.shape[:-1] + (128 - v.shape[-1],), v.dtype)
        return jnp.concatenate([v[..., half:], gap, v[..., :half]], -1)

    both = jnp.stack([ring(taps), ring(taps[..., ::-1])], 2)
    both = both.reshape(taps.shape[0], 4, 128).astype(F32)
    return jnp.pad(both, ((0, 0), (0, 4), (0, 0)))


def stamp_order(stamp_patch, stamp_band):
    z, x = place_on_torus()
    dz = lax.rem(stamp_patch // 4 - z + 4, 4)
    dx = lax.rem(lax.rem(stamp_patch, 4) - x + 4, 4)
    offset = dz * 4 + dx
    unit = jnp.zeros_like(offset)
    for number, (a, b) in enumerate(UNITS):
        unit = jnp.where(offset == (a % 4) * 4 + b % 4, number, unit)
    tile = unit * BANDS + stamp_band
    number = jnp.arange(STAMPS, dtype=jnp.int32)
    rank = tile * STAMPS + number
    before = rank[None, :] < rank[:, None]
    spot = jnp.sum(before.astype(jnp.int32), 1)
    mate = jnp.any(before & (tile[None, :] == tile[:, None]), 1).astype(jnp.int32)
    here = spot[None, :] == number[:, None]
    packed = (tile * STAMPS + number) * 2 + mate
    packed = jnp.sum(jnp.where(here, packed[None, :], 0), 1)
    tiles, ids, same = packed // (2 * STAMPS), lax.rem(packed // 2, STAMPS), lax.rem(packed, 2).astype(F32)
    every = jnp.arange(TILES, dtype=jnp.int32)
    upto = jnp.sum((tile[None, :] <= every[:, None]).astype(jnp.int32), 1)
    has = jnp.any(tile[None, :] == every[:, None], 1).astype(F32)
    return ids, tiles, same, jnp.maximum(upto - 1, 0), has


def build(row, dst):
    ring = pltpu.roll(jnp.broadcast_to(row, (128, 128)), 0, 1, stride=1, stride_axis=0)
    d = lax.broadcasted_iota(jnp.int32, (128, 128), 1) - lax.broadcasted_iota(
        jnp.int32, (128, 128), 0
    )
    zero = jnp.zeros_like(ring)
    diag = jnp.where(jnp.abs(d) < 64, ring, zero).astype(BF16)
    dst[0:128, 0:128] = diag
    dst[128:256, 128:256] = diag
    dst[112:128, 128:256] = jnp.where(d < -64, ring, zero)[112:].astype(BF16)
    dst[128:144, 0:128] = jnp.where(d > 64, ring, zero)[:16].astype(BF16)


def dot(a, b):
    return jnp.dot(a, b, preferred_element_type=F32)


def send(link, src, dst, send_sem, recv_sem):
    return pltpu.make_async_remote_copy(
        src_ref=src,
        dst_ref=dst,
        send_sem=send_sem,
        recv_sem=recv_sem,
        device_id={"patch": neighbour(LINKS[link])},
        device_id_type=MESH,
    )


def span(offset, half):
    first = UNIT[offset] * BANDS + half * HALF
    return slice(first, first + HALF)


def whole(offset):
    return slice(UNIT[offset] * BANDS, UNIT[offset] * BANDS + BANDS)


def flip(offset):
    return tuple(d if d == 2 else -d for d in offset)


def gather_copies(got, ssem, rsem):
    table = []
    for k, link in enumerate(LINKS):
        dz, dx = link
        along_x, sign = dz == 0, dz + dx
        back = flip(link)
        moves = [((0, 0), back, 0), ((0, 0), back, 1)]
        moves.append((back, (0, 2) if along_x else (2, 0), 0 if sign > 0 else 1))
        diag = []
        for s in (-sign, sign):
            diag.append(((s, 0), (s, -dx), 1) if along_x else ((0, s), (-dz, s), 0))
        far = ((2, 0), (2, -dx)) if along_x else ((0, 2), (-dz, 2))
        moves += [diag[0], (*far, 0), (*far, 1), diag[1]]
        row = [
            send(k, got.at[span(a, h)], got.at[span(b, h)], ssem.at[k, n], rsem.at[k, n])
            for n, (a, b, h) in enumerate(moves)
        ]
        rows = slice(k * 64, k * 64 + 64)
        row.append(
            send(k, got.at[whole(far[1]), rows], got.at[whole((2, 2)), rows], ssem.at[k, 7], rsem.at[k, 7])
        )
        table.append(row)
    return table


def main_kernel(ids, tls, same, last, has, gain, weight, rows, sky, pix, out, sq,
                got, tiles, pixv, seg, carry, mats, blur, resi, back, skyb,
                lsem, ssem, rsem, ssem2, rsem2, free):
    barrier = pltpu.get_barrier_semaphore()
    for link in LINKS:
        pl.semaphore_signal(
            barrier, inc=1, device_id={"patch": neighbour(link)}, device_id_type=MESH
        )
    sky_load = pltpu.make_async_copy(sky, skyb, lsem.at[0])
    sky_load.start()
    pix_load = pltpu.make_async_copy(pix, pixv, lsem.at[1])
    pix_load.start()
    sky_load.wait()

    @pl.loop(0, BANDS)
    def _(b):
        half = skyb[b].astype(BF16)
        got[b] = half
        tiles[b] = half

    pl.semaphore_wait(barrier, 4)
    moves = gather_copies(got, ssem, rsem)
    for k, link in enumerate(LINKS):
        for n in (0, 1) if sum(link) > 0 else (1, 0):
            moves[k][n].start()
    carry[...] = jnp.zeros_like(carry)
    mats[...] = jnp.zeros_like(mats)

    def keep(*offsets):
        for offset in offsets:

            @pl.loop(UNIT[offset] * BANDS, UNIT[offset] * BANDS + BANDS)
            def _(t):
                tiles[t] = got[t]

    def body(step, nothing):
        at = [step * PER + u for u in range(PER)]
        idx = [ids[a] for a in at]
        for u in range(PER):
            for m in range(4):
                build(rows[idx[u], m : m + 1, :], mats.at[u, m])
        g = [gain[i] for i in idx]
        w = [weight[i] for i in idx]
        for u in range(PER):
            blur[u] = dot(tiles[tls[at[u]]], mats[u, 3]).astype(BF16)
        for u in range(PER):
            predicted = g[u] * dot(mats[u, 0], blur[u])
            resi[u] = (w[u] * (predicted - pixv[idx[u]].astype(F32))).astype(BF16)
        for u in range(PER):
            back[u] = dot(mats[u, 1], resi[u]).astype(BF16)
        for u in range(PER):
            total = carry[...] * same[at[u]] + g[u] * dot(back[u], mats[u, 2])
            carry[...] = total
            seg[at[u]] = total.astype(BF16)
        return nothing

    def stamps(lo, hi):
        lax.fori_loop(lo // PER, hi // PER, body, 0)

    for k, link in enumerate(LINKS):
        moves[k][0 if sum(link) > 0 else 1].wait_recv()
    for k in range(4):
        moves[k][2].start()
    for k, link in enumerate(LINKS):
        moves[k][1 if sum(link) > 0 else 0].wait_recv()
    for k in range(4):
        moves[k][3].start()
    keep(*UNITS[1:5])
    pix_load.wait()
    for k in range(4):
        moves[k][2].wait_recv()
    for k in range(4):
        for n in (4, 5, 6):
            moves[k][n].start()
    keep(*UNITS[5:7])
    stamps(0, 20)
    for k in range(4):
        moves[k][3].wait_recv()
    keep(*UNITS[7:9])
    stamps(20, 44)
    for k in range(4):
        moves[k][4].wait_recv()
        moves[k][5].wait_recv()
        moves[k][7].start()
    keep(*UNITS[9:13])
    stamps(44, 92)
    for k in range(4):
        moves[k][6].wait_recv()
        moves[k][7].wait_recv()
    keep(*UNITS[13:16])
    for k in range(4):
        for n in range(8):
            moves[k][n].wait_send()
    for link in LINKS:
        pl.semaphore_signal(free, inc=1, device_id={"patch": neighbour(link)}, device_id_type=MESH)
    stamps(92, 128)

    def collect(lo, hi):
        @pl.loop(lo * BANDS, hi * BANDS)
        def _(t):
            tiles[t] = (seg[last[t]].astype(F32) * has[t]).astype(BF16)

    copies, info = [], []
    for k, link in enumerate(LINKS):
        dz, dx = link
        late = 0 if dz + dx > 0 else 1
        early = 1 - late
        along_x = dz == 0
        far = (2, dx) if along_x else (dz, 2)
        straight = (0, 2) if along_x else (2, 0)
        sides = [(s, dx) if along_x else (dz, s) for s in (1, -1)]
        diag_half = 1 if along_x else 0
        rows_k = slice(k * 64, k * 64 + 64)
        diag, three, two, one = 6 + 6 * k, 30 + 6 * k, 54 + 3 * k, 66 + 6 * k
        row = [send(k, tiles.at[whole((2, 2)), rows_k], got.at[0:6, rows_k], ssem2.at[k, 0], rsem2.at[k, 0])]
        for n, (offset, h, dst) in enumerate(
            [
                (sides[0], diag_half, diag),
                (far, 0, three),
                (far, 1, three + 3),
                (sides[1], diag_half, diag + 3),
                (straight, late, two),
                (link, early, one + early * 3),
                (link, late, one + late * 3),
            ],
            1,
        ):
            row.append(send(k, tiles.at[span(offset, h)], got.at[dst : dst + 3], ssem2.at[k, n], rsem2.at[k, n]))
        copies.append(row)
        info.append((far, straight, sides, diag_half, early, late, diag, three, two, one))

    def add_into(slots, src):
        @pl.loop(0, HALF)
        def _(t):
            d = slots.start + t
            tiles[d] = (tiles[d].astype(F32) + got[src + t].astype(F32)).astype(BF16)

    collect(15, 16)
    pl.semaphore_wait(free, 4)
    for k in range(4):
        copies[k][0].start()
    collect(7, 15)
    for k in range(4):
        copies[k][1].start()
    for k in range(4):
        copies[k][0].wait_recv()
        first = UNIT[info[k][0]] * BANDS

        @pl.loop(0, BANDS)
        def _(b):
            r = slice(k * 64, k * 64 + 64)
            tiles[first + b, r] = (tiles[first + b, r].astype(F32) + got[b, r].astype(F32)).astype(BF16)

        for n in (2, 3, 4):
            copies[k][n].start()
    collect(0, 7)
    for h in range(2):
        for k in range(4):
            copies[k][2 + h].wait_recv()
            target = (2, 0) if LINKS[k][0] == 0 else (0, 2)
            add_into(span(target, h), info[k][7] + h * HALF)
        for k in range(4):
            if info[k][5] == h:
                copies[k][5].start()
    for k in range(4):
        sides, diag_half = info[k][2:4]
        for s in range(2):
            copies[k][1 if s == 0 else 4].wait_recv()
            dz, dx = sides[s]
            target = (dz, 0) if LINKS[k][0] == 0 else (0, dx)
            add_into(span(target, diag_half), info[k][6] + s * HALF)
    for k in range(4):
        copies[k][6].start()
    for k in range(4):
        copies[k][5].wait_recv()
        add_into(span(LINKS[k], info[k][5]), info[k][8])
        copies[k][7].start()
    for k in range(4):
        copies[k][6].wait_recv()
        copies[k][7].wait_recv()

    def finish(b, total):
        gradient = tiles[b].astype(F32)
        for k in range(4):
            gradient = gradient + got[info[k][9] + b].astype(F32)
        step_field = STEP_RATE * gradient
        skyb[b] = skyb[b] - step_field
        squares = (step_field * step_field).reshape(TS // 8, 8, TS).sum(0)
        return total + squares[:, :128] + squares[:, 128:]

    sq[...] = lax.fori_loop(0, BANDS, finish, jnp.zeros((8, 128), F32))
    c = pltpu.make_async_copy(skyb, out, lsem.at[0])
    c.start()
    for k in range(4):
        for c2 in copies[k]:
            c2.wait_send()
    c.wait()


def step(order, gain, weight, rows, sky, pix):
    smem = pl.BlockSpec(memory_space=pltpu.SMEM)
    anys = pl.BlockSpec(memory_space=pl.ANY)
    vmem = pl.BlockSpec(memory_space=pltpu.VMEM)
    return pl.pallas_call(
        main_kernel,
        out_shape=(
            jax.ShapeDtypeStruct((BANDS, TS, TS), F32),
            jax.ShapeDtypeStruct((8, 128), F32),
        ),
        in_specs=[smem] * 7 + [vmem, anys, anys],
        out_specs=(anys, vmem),
        scratch_shapes=[
            pltpu.VMEM((TILES, TS, TS), BF16),
            pltpu.VMEM((TILES, TS, TS), BF16),
            pltpu.VMEM((STAMPS, TS, TS), BF16),
            pltpu.VMEM((STAMPS, TS, TS), BF16),
            pltpu.VMEM((TS, TS), F32),
            pltpu.VMEM((PER, 4, TS, TS), BF16),
            pltpu.VMEM((PER, TS, TS), BF16),
            pltpu.VMEM((PER, TS, TS), BF16),
            pltpu.VMEM((PER, TS, TS), BF16),
            pltpu.VMEM((BANDS, TS, TS), F32),
            pltpu.SemaphoreType.DMA((2,)),
            pltpu.SemaphoreType.DMA((4, 8)),
            pltpu.SemaphoreType.DMA((4, 8)),
            pltpu.SemaphoreType.DMA((4, 8)),
            pltpu.SemaphoreType.DMA((4, 8)),
            pltpu.SemaphoreType.REGULAR,
        ],
        compiler_params=pltpu.CompilerParams(
            collective_id=1, has_side_effects=True, vmem_limit_bytes=63 * 2**20 + 2**19
        ),
        name="step",
    )(*order, gain, weight, rows, sky, pix)


def total_kernel(sq, out, held, ssem, rsem):
    patch, exp = lax.axis_index("patch"), lax.axis_index("exp")
    z, x = patch // 4, lax.rem(patch, 4)
    y, core = exp // 2, lax.rem(exp, 2)
    rounds = [
        (core, [("exp", exp + 1 - 2 * core)]),
        (x, [("patch", z * 4 + lax.rem(x + d, 4)) for d in (1, 2, 3)]),
        (z, [("patch", lax.rem(z + d, 4) * 4 + x) for d in (1, 2, 3)]),
        (y, [("exp", lax.rem(y + d, 4) * 2 + core) for d in (1, 2, 3)]),
    ]
    barrier = pltpu.get_barrier_semaphore()
    for _, peers in rounds:
        for peer in peers:
            pl.semaphore_signal(barrier, inc=1, device_id=dict([peer]), device_id_type=MESH)
    total = jnp.sum(sq[...], 0, keepdims=True)
    total = jnp.broadcast_to(total, (8, 128))
    pl.semaphore_wait(barrier, 10)
    for n, (place, peers) in enumerate(rounds):
        held[n, place] = total
        copies = [
            pltpu.make_async_remote_copy(
                src_ref=held.at[n, place], dst_ref=held.at[n, place],
                send_sem=ssem.at[n, k], recv_sem=rsem.at[n, k],
                device_id=dict([peer]), device_id_type=MESH,
            )
            for k, peer in enumerate(peers)
        ]
        for c in copies:
            c.start()
        for c in copies:
            c.wait()
        total = held[n, 0]
        for k in range(1, len(peers) + 1):
            total = total + held[n, k]
    total = jnp.sum(total[0:1], 1, keepdims=True)
    count = 16 * 8 * BANDS * TS * TS
    out[...] = jnp.broadcast_to(jnp.sqrt(total / count + 1e-06), (8, 128))


def total_of(sq):
    vmem = pl.BlockSpec(memory_space=pltpu.VMEM)
    return pl.pallas_call(
        total_kernel,
        out_shape=jax.ShapeDtypeStruct((8, 128), F32),
        in_specs=[vmem],
        out_specs=vmem,
        scratch_shapes=[
            pltpu.VMEM((4, 4, 8, 128), F32),
            pltpu.SemaphoreType.DMA((4, 3)),
            pltpu.SemaphoreType.DMA((4, 3)),
        ],
        compiler_params=pltpu.CompilerParams(collective_id=2, has_side_effects=True),
        name="total",
    )(sq)


def per_device(
    sky_model, stamp_pixels, stamp_patch, stamp_band, psf_taps, stamp_gain, stamp_weight
):
    sky = sky_model.reshape(BANDS, TS, TS)
    order = stamp_order(stamp_patch[:, 0], stamp_band)
    rows = tap_rows(psf_taps)
    gain, weight = stamp_gain.astype(F32), stamp_weight.astype(F32)
    new_model, squares = step(order, gain, weight, rows, sky, stamp_pixels)
    return (new_model.reshape(sky_model.shape), total_of(squares)[0, 0])


def solution(mesh):
    return jax.shard_map(
        per_device,
        mesh=mesh,
        in_specs=(
            P("patch", "exp", None, None, None),
            P(("patch", "exp"), None, None),
            P(("patch", "exp"), None),
            P(("patch", "exp")),
            P(("patch", "exp"), None, None),
            P(("patch", "exp")),
            P(("patch", "exp")),
        ),
        out_specs=(P("patch", "exp", None, None, None), P()),
        check_vma=False,
    )
```

```python
import functools

import jax
import jax.numpy as jnp
from jax import lax
from jax.experimental import pallas as pl
from jax.experimental.pallas import tpu as pltpu
from jax.sharding import PartitionSpec as P

TS = 256
BANDS = 6
HALF = 3
STAMPS = 128
STEP_RATE = 0.2
F32, BF16 = jnp.float32, jnp.bfloat16
MESH = pl.DeviceIdType.MESH

UNITS = [
    (0, 0), (0, 1), (0, -1), (1, 0), (-1, 0),
    (1, -1), (-1, 1), (0, 2), (2, 0), (1, 1), (-1, -1),
    (2, 1), (1, 2), (2, -1), (-1, 2), (2, 2),
]
UNIT = {offset: number for number, offset in enumerate(UNITS)}
TILES = len(UNITS) * BANDS
LINKS = [(0, 1), (0, -1), (1, 0), (-1, 0)]
PER = 4


def place_on_torus():
    patch = lax.axis_index("patch")
    return patch // 4, lax.rem(patch, 4)


def neighbour(offset):
    z, x = place_on_torus()
    return lax.rem(z + offset[0] + 4, 4) * 4 + lax.rem(x + offset[1] + 4, 4)


def index_grids():
    return (
        lax.broadcasted_iota(jnp.int32, (128, 128), 0),
        lax.broadcasted_iota(jnp.int32, (128, 128), 1),
    )


def tap_rows(taps, rows):
    source, lane = index_grids()
    tap = jnp.where(lane <= 10, lane + 10, lane - 118)
    used = (lane <= 10) | (lane >= 118)
    for m in range(4):
        wanted = (20 - tap if m % 2 else tap) + 21 * (m // 2)
        pick = jnp.where(used & (source == wanted), 1.0, 0.0).astype(BF16)
        rows[m] = dot(taps[...], pick)


def stamp_order(patch, band, gain, weight, ints, floats):
    z, x = place_on_torus()
    down, lane = index_grids()

    def across(line):
        return jnp.broadcast_to(line, (128, 128))

    def total(grid):
        return jnp.sum(grid, 0, keepdims=True)

    where = across(patch[...])
    dz = lax.rem(where // 4 - z + 4, 4)
    dx = lax.rem(lax.rem(where, 4) - x + 4, 4)
    offset = dz * 4 + dx
    unit = jnp.zeros_like(offset)
    for number, (a, b) in enumerate(UNITS):
        unit = jnp.where(offset == (a % 4) * 4 + b % 4, number, unit)
    tile_d = unit * BANDS + across(band[...]).T
    tile_l = tile_d.T
    rank_d, rank_l = tile_d * STAMPS + down, tile_l * STAMPS + lane
    before = rank_d < rank_l
    one, none = jnp.ones_like(down), jnp.zeros_like(down)
    spot = across(total(jnp.where(before, one, none))).T
    mates = across(total(jnp.where(before & (tile_d == tile_l), one, none))).T
    here = spot == lane
    ints[0:1, :] = total(jnp.where(here, down, none))
    ints[1:2, :] = total(jnp.where(here, tile_d, none))
    ints[2:3, :] = jnp.maximum(total(jnp.where(tile_d <= lane, one, none)) - 1, 0)
    zero = jnp.zeros((128, 128), F32)
    floats[0:1, :] = total(jnp.where(here & (mates > 0), zero + 1.0, zero))
    floats[1:2, :] = jnp.where(total(jnp.where(tile_d == lane, one, none)) > 0, 1.0, 0.0)
    floats[2:3, :] = total(jnp.where(here, across(gain[...].astype(F32)).T, zero))
    floats[3:4, :] = total(jnp.where(here, across(weight[...].astype(F32)).T, zero))


def build(row, dst):
    ring = pltpu.roll(jnp.broadcast_to(row, (128, 128)), 0, 1, stride=1, stride_axis=0)
    d = lax.broadcasted_iota(jnp.int32, (128, 128), 1) - lax.broadcasted_iota(
        jnp.int32, (128, 128), 0
    )
    zero = jnp.zeros_like(ring)
    diag = jnp.where(jnp.abs(d) < 64, ring, zero).astype(BF16)
    dst[0:128, 0:128] = diag
    dst[128:256, 128:256] = diag
    dst[112:128, 128:256] = jnp.where(d < -64, ring, zero)[112:].astype(BF16)
    dst[128:144, 0:128] = jnp.where(d > 64, ring, zero)[:16].astype(BF16)


def dot(a, b):
    return jnp.dot(a, b, preferred_element_type=F32)


def send(link, src, dst, send_sem, recv_sem):
    return pltpu.make_async_remote_copy(
        src_ref=src,
        dst_ref=dst,
        send_sem=send_sem,
        recv_sem=recv_sem,
        device_id={"patch": neighbour(LINKS[link])},
        device_id_type=MESH,
    )


def span(offset, half):
    first = UNIT[offset] * BANDS + half * HALF
    return slice(first, first + HALF)


def whole(offset):
    return slice(UNIT[offset] * BANDS, UNIT[offset] * BANDS + BANDS)


def seen_from(link, offset):
    dz, dx = ((a - b + 1) % 4 - 1 for a, b in zip(offset, link))
    return dz, dx


FAR = [
    [((1, -1), 1), ((2, 0), 0)],
    [((2, 0), 0), ((-1, 1), 1)],
    [((-1, 1), 1), ((0, 2), 0)],
    [((0, 2), 0), ((1, -1), 1)],
]


def gather_copies(got, ssem, rsem):
    table = []
    for k, link in enumerate(LINKS):
        dz, dx = link
        along_x, sign = dz == 0, dz + dx
        diag = [((s, 0), 1) if along_x else ((0, s), 0) for s in (sign, -sign)]
        straight = ((-dz, -dx), 0 if sign > 0 else 1)
        moves = [((0, 0), 0), ((0, 0), 1), diag[0], straight, diag[1], *FAR[k]]
        row = [
            send(k, got.at[span(a, h)], got.at[span(seen_from(link, a), h)], ssem.at[k, n], rsem.at[k, n])
            for n, (a, h) in enumerate(moves)
        ]
        rows = slice(k * 64, k * 64 + 64)
        via = (2, -dx) if along_x else (-dz, 2)
        row.append(
            send(k, got.at[whole(via), rows], got.at[whole((2, 2)), rows], ssem.at[k, 7], rsem.at[k, 7])
        )
        table.append(row)
    return table


def reduce_copies(tiles, got, ssem, rsem):
    copies, info = [], []
    for k, link in enumerate(LINKS):
        dz, dx = link
        late = 0 if dz + dx > 0 else 1
        early = 1 - late
        along_x = dz == 0
        far = (2, dx) if along_x else (dz, 2)
        straight = (0, 2) if along_x else (2, 0)
        sides = [(s, dx) if along_x else (dz, s) for s in (-dz - dx, dz + dx)]
        diag_half = 1 if along_x else 0
        rows_k = slice(k * 64, k * 64 + 64)
        diag, three, two, one = 6 + 6 * k, 30 + 6 * k, 54 + 3 * k, 66 + 6 * k
        row = [send(k, tiles.at[whole((2, 2)), rows_k], got.at[0:6, rows_k], ssem.at[k, 0], rsem.at[k, 0])]
        for n, (offset, h, dst) in enumerate(
            [
                (sides[0], diag_half, diag),
                (far, 0, three),
                (far, 1, three + 3),
                (sides[1], diag_half, diag + 3),
                (straight, late, two),
                (link, early, one + early * 3),
                (link, late, one + late * 3),
            ],
            1,
        ):
            row.append(send(k, tiles.at[span(offset, h)], got.at[dst : dst + 3], ssem.at[k, n], rsem.at[k, n]))
        copies.append(row)
        info.append((far, straight, sides, diag_half, early, late, diag, three, two, one))

    return copies, info


def main_kernel(patch_of, band_of, gain_of, weight_of, taps, sky, pix, out, rms,
                got, tiles, pixv, seg, carry, mats, blur, resi, back, skyb, rows, intv, floatv, ints, floats, held, held2,
                lsem, ssem, rsem, ssem2, rsem2, tsem, tsem2, tsem3, tsem4, early, free):
    patch, exp = lax.axis_index("patch"), lax.axis_index("exp")
    peers = [{"patch": lax.rem(patch + k, 16)} for k in range(1, 16)]
    peers2 = [{"exp": lax.rem(exp + k, 8)} for k in range(1, 8)]
    barrier = pltpu.get_barrier_semaphore()
    for peer in peers + peers2:
        pl.semaphore_signal(barrier, inc=1, device_id=peer, device_id_type=MESH)
    sky_load = pltpu.make_async_copy(sky, skyb, lsem.at[0])
    sky_load.start()
    pix_load = pltpu.make_async_copy(pix, pixv, lsem.at[1])
    pix_load.start()
    sky_load.wait()

    @pl.loop(0, BANDS)
    def _(b):
        half = skyb[b].astype(BF16)
        got[b] = half
        tiles[b] = half

    pl.semaphore_wait(barrier, len(peers) + len(peers2))
    moves = gather_copies(got, ssem, rsem)
    for k, link in enumerate(LINKS):
        for n in (0, 1) if link[0] == 0 else (1, 0):
            moves[k][n].start()
    stamp_order(patch_of, band_of, gain_of, weight_of, intv, floatv)
    tables = [
        pltpu.make_async_copy(intv, ints, lsem.at[2]),
        pltpu.make_async_copy(floatv, floats, lsem.at[3]),
    ]
    for c in tables:
        c.start()
    tap_rows(taps, rows)
    carry[...] = jnp.zeros_like(carry)
    mats[...] = jnp.zeros_like(mats)

    def keep(*offsets):
        for offset in offsets:

            @pl.loop(UNIT[offset] * BANDS, UNIT[offset] * BANDS + BANDS)
            def _(t):
                tiles[t] = got[t]

    def body(step, nothing):
        at = [step * PER + u for u in range(PER)]
        idx = [ints[0, a] for a in at]
        for u in range(PER):
            for m in range(4):
                build(rows[m, pl.ds(idx[u], 1), :], mats.at[u, m])
        g = [floats[2, a] for a in at]
        w = [floats[3, a] for a in at]
        for u in range(PER):
            blur[u] = dot(tiles[ints[1, at[u]]], mats[u, 3]).astype(BF16)
        for u in range(PER):
            predicted = g[u] * dot(mats[u, 0], blur[u])
            resi[u] = (w[u] * (predicted - pixv[idx[u]].astype(F32))).astype(BF16)
        for u in range(PER):
            back[u] = dot(mats[u, 1], resi[u]).astype(BF16)
        for u in range(PER):
            total = carry[...] * floats[0, at[u]] + g[u] * dot(back[u], mats[u, 2])
            carry[...] = total
            seg[at[u]] = total.astype(BF16)
        return nothing

    def stamps(lo, hi):
        lax.fori_loop(lo // PER, hi // PER, body, 0)

    def collect(lo, hi):
        @pl.loop(lo * BANDS, hi * BANDS)
        def _(t):
            tiles[t] = (seg[ints[2, t]].astype(F32) * floats[1, t]).astype(BF16)

    def tell(semaphore):
        for link in LINKS:
            pl.semaphore_signal(
                semaphore, inc=1, device_id={"patch": neighbour(link)}, device_id_type=MESH
            )

    copies, info = reduce_copies(tiles, got, ssem2, rsem2)

    def arrive(*numbers):
        for k in range(4):
            for n in numbers:
                moves[k][n].wait_recv()

    def forward(*numbers):
        for k in range(4):
            for n in numbers:
                moves[k][n].start()

    def gone(*numbers):
        for k in range(4):
            for n in numbers:
                moves[k][n].wait_send()

    for k, link in enumerate(LINKS):
        moves[k][0 if link[0] == 0 else 1].wait_recv()
    forward(2)
    for k, link in enumerate(LINKS):
        moves[k][1 if link[0] == 0 else 0].wait_recv()
    forward(3, 4)
    keep(*UNITS[1:5])
    for c in tables:
        c.wait()
    pix_load.wait()
    arrive(2)
    keep(*UNITS[5:7])
    stamps(0, 20)
    arrive(3)
    forward(5, 6)
    keep(*UNITS[7:9])
    stamps(20, 44)
    arrive(4)
    keep(*UNITS[9:11])
    stamps(44, 68)
    arrive(5)
    for k in (1, 3):
        moves[k][7].start()
    keep(*UNITS[11:13])
    gone(2, 3, 4)
    tell(early)
    stamps(68, 92)
    arrive(6)
    for k in (0, 2):
        moves[k][7].start()
    keep(*UNITS[13:15])
    collect(5, 7)
    pl.semaphore_wait(early, 4)
    for k in range(4):
        copies[k][1].start()
    stamps(92, 116)
    arrive(7)
    keep(*UNITS[15:16])
    gone(0, 1, 5, 6, 7)
    tell(free)
    stamps(116, 128)

    def add_into(slots, src):
        @pl.loop(0, HALF)
        def _(t):
            d = slots.start + t
            tiles[d] = (tiles[d].astype(F32) + got[src + t].astype(F32)).astype(BF16)

    collect(15, 16)
    pl.semaphore_wait(free, 4)
    for k in range(4):
        copies[k][0].start()
    collect(9, 15)
    for k in range(4):
        copies[k][0].wait_recv()
        first = UNIT[info[k][0]] * BANDS

        @pl.loop(0, BANDS)
        def _(b):
            r = slice(k * 64, k * 64 + 64)
            tiles[first + b, r] = (tiles[first + b, r].astype(F32) + got[b, r].astype(F32)).astype(BF16)

        for n in (2, 3, 4):
            copies[k][n].start()
    collect(0, 5)
    collect(7, 9)
    for h in range(2):
        for k in range(4):
            copies[k][2 + h].wait_recv()
            target = (2, 0) if LINKS[k][0] == 0 else (0, 2)
            add_into(span(target, h), info[k][7] + h * HALF)
        for k in range(4):
            if info[k][5] == h:
                copies[k][5].start()
    for k in range(4):
        sides, diag_half = info[k][2:4]
        for s in range(2):
            copies[k][1 if s == 0 else 4].wait_recv()
            dz, dx = sides[s]
            target = (dz, 0) if LINKS[k][0] == 0 else (0, dx)
            add_into(span(target, diag_half), info[k][6] + s * HALF)
    for k in range(4):
        copies[k][6].start()
    for k in range(4):
        copies[k][5].wait_recv()
        add_into(span(LINKS[k], info[k][5]), info[k][8])
        copies[k][7].start()
    for k in range(4):
        copies[k][6].wait_recv()
        copies[k][7].wait_recv()

    def finish(b, total):
        gradient = tiles[b].astype(F32)
        for k in range(4):
            gradient = gradient + got[info[k][9] + b].astype(F32)
        step_field = STEP_RATE * gradient
        skyb[b] = skyb[b] - step_field
        squares = (step_field * step_field).reshape(TS // 8, 8, TS).sum(0)
        return total + squares[:, :128] + squares[:, 128:]

    squares = lax.fori_loop(0, BANDS, finish, jnp.zeros((8, 128), F32))
    c = pltpu.make_async_copy(skyb, out, lsem.at[0])
    c.start()

    def exchange(slots, place, value, devices, send_sems, recv_sems):
        slots[place] = value
        shares = [
            pltpu.make_async_remote_copy(
                src_ref=slots.at[place],
                dst_ref=slots.at[place],
                send_sem=send_sems.at[k],
                recv_sem=recv_sems.at[k],
                device_id=device,
                device_id_type=MESH,
            )
            for k, device in enumerate(devices)
        ]
        for share in shares:
            share.start()
        for share in shares:
            share.wait()
        return jnp.sum(slots[...], 0)

    squares = exchange(held, patch, squares, peers, tsem, tsem2)
    squares = exchange(held2, exp, squares, peers2, tsem3, tsem4)
    mean = jnp.sum(jnp.sum(squares, 0, keepdims=True), 1, keepdims=True) / (128 * BANDS * TS * TS)
    rms[...] = jnp.broadcast_to(jnp.sqrt(mean + 1e-06), rms.shape)
    for k in range(4):
        for c2 in copies[k]:
            c2.wait_send()
    c.wait()


def step(patch, band, gain, weight, taps, sky, pix):
    anys = pl.BlockSpec(memory_space=pl.ANY)
    vmem = pl.BlockSpec(memory_space=pltpu.VMEM)
    return pl.pallas_call(
        main_kernel,
        out_shape=(
            jax.ShapeDtypeStruct((BANDS, TS, TS), F32),
            jax.ShapeDtypeStruct((1, 128), F32),
        ),
        in_specs=[vmem] * 5 + [anys, anys],
        out_specs=(anys, vmem),
        scratch_shapes=[
            pltpu.VMEM((TILES, TS, TS), BF16),
            pltpu.VMEM((TILES, TS, TS), BF16),
            pltpu.VMEM((STAMPS, TS, TS), BF16),
            pltpu.VMEM((STAMPS, TS, TS), BF16),
            pltpu.VMEM((TS, TS), F32),
            pltpu.VMEM((PER, 4, TS, TS), BF16),
            pltpu.VMEM((PER, TS, TS), BF16),
            pltpu.VMEM((PER, TS, TS), BF16),
            pltpu.VMEM((PER, TS, TS), BF16),
            pltpu.VMEM((BANDS, TS, TS), F32),
            pltpu.VMEM((4, 128, 128), F32),
            pltpu.VMEM((8, 128), jnp.int32),
            pltpu.VMEM((8, 128), F32),
            pltpu.SMEM((8, 128), jnp.int32),
            pltpu.SMEM((8, 128), F32),
            pltpu.VMEM((16, 8, 128), F32),
            pltpu.VMEM((8, 8, 128), F32),
            pltpu.SemaphoreType.DMA((4,)),
            pltpu.SemaphoreType.DMA((4, 8)),
            pltpu.SemaphoreType.DMA((4, 8)),
            pltpu.SemaphoreType.DMA((4, 8)),
            pltpu.SemaphoreType.DMA((4, 8)),
            pltpu.SemaphoreType.DMA((15,)),
            pltpu.SemaphoreType.DMA((15,)),
            pltpu.SemaphoreType.DMA((7,)),
            pltpu.SemaphoreType.DMA((7,)),
            pltpu.SemaphoreType.REGULAR,
            pltpu.SemaphoreType.REGULAR,
        ],
        compiler_params=pltpu.CompilerParams(
            collective_id=1, has_side_effects=True, vmem_limit_bytes=63 * 2**20 + 2**19
        ),
        name="step",
    )(patch, band, gain, weight, taps, sky, pix)


def per_device(
    sky_model, stamp_pixels, stamp_patch, stamp_band, psf_taps, stamp_gain, stamp_weight
):
    sky = sky_model.reshape(BANDS, TS, TS)
    taps = jnp.pad(psf_taps.reshape(STAMPS, -1), ((0, 0), (0, 128 - 2 * psf_taps.shape[-1])))
    band, gain, weight = (v.reshape(1, STAMPS) for v in (stamp_band, stamp_gain, stamp_weight))
    new_model, rms = step(stamp_patch, band, gain, weight, taps, sky, stamp_pixels)
    return (new_model.reshape(sky_model.shape), rms[0, 0])


def solution(mesh):
    return jax.shard_map(
        per_device,
        mesh=mesh,
        in_specs=(
            P("patch", "exp", None, None, None),
            P(("patch", "exp"), None, None),
            P(("patch", "exp"), None),
            P(("patch", "exp")),
            P(("patch", "exp"), None, None),
            P(("patch", "exp")),
            P(("patch", "exp")),
        ),
        out_specs=(P("patch", "exp", None, None, None), P()),
        check_vma=False,
    )
```

```python
import functools

import jax
import jax.numpy as jnp
from jax import lax
from jax.experimental import pallas as pl
from jax.experimental.pallas import tpu as pltpu
from jax.sharding import PartitionSpec as P

TS = 256
BANDS = 6
HALF = 3
STAMPS = 128
STEP_RATE = 0.2
F32, BF16 = jnp.float32, jnp.bfloat16
MESH = pl.DeviceIdType.MESH

UNITS = [
    (0, 0), (0, 1), (0, -1), (1, 0), (-1, 0),
    (1, -1), (-1, 1), (0, 2), (2, 0), (1, 1), (-1, -1),
    (2, 1), (1, 2), (2, -1), (-1, 2), (2, 2),
]
UNIT = {offset: number for number, offset in enumerate(UNITS)}
TILES = len(UNITS) * BANDS
LINKS = [(0, 1), (0, -1), (1, 0), (-1, 0)]
PER = 4


def place_on_torus():
    patch = lax.axis_index("patch")
    return patch // 4, lax.rem(patch, 4)


def neighbour(offset):
    z, x = place_on_torus()
    return lax.rem(z + offset[0] + 4, 4) * 4 + lax.rem(x + offset[1] + 4, 4)


def index_grids():
    return (
        lax.broadcasted_iota(jnp.int32, (128, 128), 0),
        lax.broadcasted_iota(jnp.int32, (128, 128), 1),
    )


def tap_rows(taps, rows):
    source, lane = index_grids()
    tap = jnp.where(lane <= 10, lane + 10, lane - 118)
    used = (lane <= 10) | (lane >= 118)
    rows[0] = jnp.zeros((128, 128), F32)
    for k in range(taps.shape[0]):
        rows[0, 2 * k : 2 * k + 2, :] = taps[k].astype(F32)
    lines = rows[0].T.astype(BF16)
    for m in range(4):
        wanted = 2 * (20 - tap if m % 2 else tap) + m // 2
        pick = jnp.where(used & (source == wanted), 1.0, 0.0).astype(BF16)
        rows[m] = dot(lines, pick)


def stamp_order(patch, band, gain, weight, ints, floats):
    z, x = place_on_torus()
    down, lane = index_grids()

    def across(line):
        return jnp.broadcast_to(line, (128, 128))

    def total(grid):
        return jnp.sum(grid, 0, keepdims=True)

    where = across(patch[...]).T
    dz = lax.rem(where // 4 - z + 4, 4)
    dx = lax.rem(lax.rem(where, 4) - x + 4, 4)
    offset = dz * 4 + dx
    unit = jnp.zeros_like(offset)
    for number, (a, b) in enumerate(UNITS):
        unit = jnp.where(offset == (a % 4) * 4 + b % 4, number, unit)
    tile_d = unit * BANDS + across(band[...]).T
    tile_l = tile_d.T
    rank_d, rank_l = tile_d * STAMPS + down, tile_l * STAMPS + lane
    before = rank_d < rank_l
    one, none = jnp.ones_like(down), jnp.zeros_like(down)
    spot = across(total(jnp.where(before, one, none))).T
    mates = across(total(jnp.where(before & (tile_d == tile_l), one, none))).T
    here = spot == lane
    ints[0:1, :] = total(jnp.where(here, down, none))
    ints[1:2, :] = total(jnp.where(here, tile_d, none))
    ints[2:3, :] = jnp.maximum(total(jnp.where(tile_d <= lane, one, none)) - 1, 0)
    zero = jnp.zeros((128, 128), F32)
    floats[0:1, :] = total(jnp.where(here & (mates > 0), zero + 1.0, zero))
    floats[1:2, :] = jnp.where(total(jnp.where(tile_d == lane, one, none)) > 0, 1.0, 0.0)
    floats[2:3, :] = total(jnp.where(here, across(gain[...].astype(F32)).T, zero))
    floats[3:4, :] = total(jnp.where(here, across(weight[...].astype(F32)).T, zero))


def build(row, dst):
    ring = pltpu.roll(jnp.broadcast_to(row, (128, 128)), 0, 1, stride=1, stride_axis=0)
    d = lax.broadcasted_iota(jnp.int32, (128, 128), 1) - lax.broadcasted_iota(
        jnp.int32, (128, 128), 0
    )
    zero = jnp.zeros_like(ring)
    diag = jnp.where(jnp.abs(d) < 64, ring, zero).astype(BF16)
    dst[0:128, 0:128] = diag
    dst[128:256, 128:256] = diag
    dst[112:128, 128:256] = jnp.where(d < -64, ring, zero)[112:].astype(BF16)
    dst[128:144, 0:128] = jnp.where(d > 64, ring, zero)[:16].astype(BF16)


def dot(a, b):
    return jnp.dot(a, b, preferred_element_type=F32)


def send(link, src, dst, send_sem, recv_sem):
    return pltpu.make_async_remote_copy(
        src_ref=src,
        dst_ref=dst,
        send_sem=send_sem,
        recv_sem=recv_sem,
        device_id={"patch": neighbour(LINKS[link])},
        device_id_type=MESH,
    )


def span(offset, half):
    first = UNIT[offset] * BANDS + half * HALF
    return slice(first, first + HALF)


def whole(offset):
    return slice(UNIT[offset] * BANDS, UNIT[offset] * BANDS + BANDS)


def seen_from(link, offset):
    dz, dx = ((a - b + 1) % 4 - 1 for a, b in zip(offset, link))
    return dz, dx


FAR = [
    [((1, -1), 1), ((2, 0), 0)],
    [((2, 0), 0), ((-1, 1), 1)],
    [((-1, 1), 1), ((0, 2), 0)],
    [((0, 2), 0), ((1, -1), 1)],
]


def gather_copies(got, ssem, rsem):
    table = []
    for k, link in enumerate(LINKS):
        dz, dx = link
        along_x, sign = dz == 0, dz + dx
        diag = [((s, 0), 1) if along_x else ((0, s), 0) for s in (sign, -sign)]
        straight = ((-dz, -dx), 0 if sign > 0 else 1)
        moves = [((0, 0), 0), ((0, 0), 1), diag[0], straight, diag[1], *FAR[k]]
        row = [
            send(k, got.at[span(a, h)], got.at[span(seen_from(link, a), h)], ssem.at[k, n], rsem.at[k, n])
            for n, (a, h) in enumerate(moves)
        ]
        rows = slice(k * 64, k * 64 + 64)
        via = (2, -dx) if along_x else (-dz, 2)
        row.append(
            send(k, got.at[whole(via), rows], got.at[whole((2, 2)), rows], ssem.at[k, 7], rsem.at[k, 7])
        )
        table.append(row)
    return table


def reduce_copies(tiles, got, ssem, rsem):
    copies, info = [], []
    for k, link in enumerate(LINKS):
        dz, dx = link
        late = 0 if dz + dx > 0 else 1
        early = 1 - late
        along_x = dz == 0
        far = (2, dx) if along_x else (dz, 2)
        straight = (0, 2) if along_x else (2, 0)
        sides = [(s, dx) if along_x else (dz, s) for s in (-dz - dx, dz + dx)]
        diag_half = 1 if along_x else 0
        rows_k = slice(k * 64, k * 64 + 64)
        diag, three, two, one = 6 + 6 * k, 30 + 6 * k, 54 + 3 * k, 66 + 6 * k
        row = [send(k, tiles.at[whole((2, 2)), rows_k], got.at[0:6, rows_k], ssem.at[k, 0], rsem.at[k, 0])]
        for n, (offset, h, dst) in enumerate(
            [
                (sides[0], diag_half, diag),
                (far, 0, three),
                (far, 1, three + 3),
                (sides[1], diag_half, diag + 3),
                (straight, late, two),
            ],
            1,
        ):
            row.append(send(k, tiles.at[span(offset, h)], got.at[dst : dst + 3], ssem.at[k, n], rsem.at[k, n]))
        for n, (tile, dst, count) in enumerate(
            [
                (span(link, early).start, one + early * 3, 2),
                (span(link, early).start + 2, one + early * 3 + 2, 1),
                (span(link, late).start, one + late * 3, 3),
            ],
            6,
        ):
            row.append(send(k, tiles.at[tile : tile + count], got.at[dst : dst + count], ssem.at[k, n], rsem.at[k, n]))
        copies.append(row)
        info.append((far, straight, sides, diag_half, early, late, diag, three, two, one))

    return copies, info


def main_kernel(patch_of, band_of, gain_of, weight_of, taps, sky, pix, out, rms,
                got, tiles, pixv, seg, carry, mats, blur, resi, skyb, rows, intv, floatv, ints, floats, held, held2,
                lsem, ssem, rsem, ssem2, rsem2, tsem, tsem2, tsem3, tsem4, early, free):
    sky_load = pltpu.make_async_copy(sky, skyb, lsem.at[0])
    sky_load.start()
    patch, exp = lax.axis_index("patch"), lax.axis_index("exp")
    peers = [{"patch": lax.rem(patch + k, 16)} for k in range(1, 16)]
    peers2 = [{"exp": lax.rem(exp + k, 8)} for k in range(1, 8)]
    barrier = pltpu.get_barrier_semaphore()
    for peer in peers + peers2:
        pl.semaphore_signal(barrier, inc=1, device_id=peer, device_id_type=MESH)
    pix_load = pltpu.make_async_copy(pix, pixv, lsem.at[1])
    sky_load.wait()
    pix_load.start()

    @pl.loop(0, BANDS)
    def _(b):
        half = skyb[b].astype(BF16)
        got[b] = half
        tiles[b] = half

    pl.semaphore_wait(barrier, len(peers) + len(peers2))
    moves = gather_copies(got, ssem, rsem)
    for k, link in enumerate(LINKS):
        for n in (0, 1) if link[0] == 0 else (1, 0):
            moves[k][n].start()
    stamp_order(patch_of, band_of, gain_of, weight_of, intv, floatv)
    tables = [
        pltpu.make_async_copy(intv, ints, lsem.at[2]),
        pltpu.make_async_copy(floatv, floats, lsem.at[3]),
    ]
    for c in tables:
        c.start()
    tap_rows(taps, rows)
    carry[...] = jnp.zeros_like(carry)
    mats[...] = jnp.zeros_like(mats)

    def keep(*offsets):
        for offset in offsets:

            @pl.loop(UNIT[offset] * BANDS, UNIT[offset] * BANDS + BANDS)
            def _(t):
                tiles[t] = got[t]

    def body(step, nothing):
        at = [step * PER + u for u in range(PER)]
        idx = [ints[0, a] for a in at]
        for u in range(PER):
            for m in range(4):
                build(rows[m, pl.ds(idx[u], 1), :], mats.at[u, m])
        g = [floats[2, a] for a in at]
        w = [floats[3, a] for a in at]
        for u in range(PER):
            blur[u] = dot(tiles[ints[1, at[u]]], mats[u, 3]).astype(BF16)
        for u in range(PER):
            predicted = g[u] * dot(mats[u, 0], blur[u])
            resi[u] = (w[u] * (predicted - pixv[idx[u]].astype(F32))).astype(BF16)
        for u in range(PER):
            blur[u] = dot(mats[u, 1], resi[u]).astype(BF16)
        for u in range(PER):
            total = carry[...] * floats[0, at[u]] + g[u] * dot(blur[u], mats[u, 2])
            carry[...] = total
            seg[at[u]] = total.astype(BF16)
        return nothing

    def stamps(lo, hi):
        lax.fori_loop(lo // PER, hi // PER, body, 0)

    def collect(lo, hi):
        @pl.loop(lo * BANDS, hi * BANDS)
        def _(t):
            tiles[t] = (seg[ints[2, t]].astype(F32) * floats[1, t]).astype(BF16)

    def tell(semaphore):
        for link in LINKS:
            pl.semaphore_signal(
                semaphore, inc=1, device_id={"patch": neighbour(link)}, device_id_type=MESH
            )

    copies, info = reduce_copies(tiles, got, ssem2, rsem2)

    def arrive(*numbers):
        for k in range(4):
            for n in numbers:
                moves[k][n].wait_recv()

    def forward(*numbers):
        for k in range(4):
            for n in numbers:
                moves[k][n].start()

    def gone(*numbers):
        for k in range(4):
            for n in numbers:
                moves[k][n].wait_send()

    for k, link in enumerate(LINKS):
        moves[k][0 if link[0] == 0 else 1].wait_recv()
    forward(2)
    for k, link in enumerate(LINKS):
        moves[k][1 if link[0] == 0 else 0].wait_recv()
    forward(3, 4)
    keep(*UNITS[1:5])
    for c in tables:
        c.wait()
    pix_load.wait()
    arrive(2)
    keep(*UNITS[5:7])
    stamps(0, 20)
    arrive(3)
    forward(5, 6)
    keep(*UNITS[7:9])
    stamps(20, 44)
    arrive(4)
    keep(*UNITS[9:11])
    stamps(44, 68)
    arrive(5)
    for k in (1, 3):
        moves[k][7].start()
    keep(*UNITS[11:13])
    gone(2, 3, 4)
    tell(early)
    stamps(68, 92)
    arrive(6)
    for k in (0, 2):
        moves[k][7].start()
    keep(*UNITS[13:15])
    collect(5, 7)
    pl.semaphore_wait(early, 4)
    for k in range(4):
        copies[k][1].start()
    stamps(92, 116)
    arrive(7)
    keep(*UNITS[15:16])
    gone(0, 1, 5, 6, 7)
    tell(free)
    stamps(116, 128)

    def add_into(slots, src):
        @pl.loop(0, HALF)
        def _(t):
            d = slots.start + t
            tiles[d] = (tiles[d].astype(F32) + got[src + t].astype(F32)).astype(BF16)

    collect(15, 16)
    pl.semaphore_wait(free, 4)
    for k in range(4):
        copies[k][0].start()
    collect(9, 11)
    for k in range(4):
        copies[k][4].start()
    collect(11, 15)
    for k in range(4):
        copies[k][0].wait_recv()
        first = UNIT[info[k][0]] * BANDS

        @pl.loop(0, BANDS)
        def _(b):
            r = slice(k * 64, k * 64 + 64)
            tiles[first + b, r] = (tiles[first + b, r].astype(F32) + got[b, r].astype(F32)).astype(BF16)

        for n in (2, 3):
            copies[k][n].start()
    collect(0, 5)
    collect(7, 9)
    for n in (1, 4):
        for k in range(4):
            sides, diag_half = info[k][2:4]
            copies[k][n].wait_recv()
            dz, dx = sides[n // 4]
            target = (dz, 0) if LINKS[k][0] == 0 else (0, dx)
            add_into(span(target, diag_half), info[k][6] + n // 4 * HALF)
    for k in range(4):
        copies[k][6].start()
    for h in range(2):
        for k in range(4):
            copies[k][2 + h].wait_recv()
            target = (2, 0) if LINKS[k][0] == 0 else (0, 2)
            add_into(span(target, h), info[k][7] + h * HALF)
        for k in range(4):
            if info[k][5] == h:
                copies[k][5].start()
                copies[k][7].start()
    for k in range(4):
        copies[k][5].wait_recv()
        add_into(span(LINKS[k], info[k][5]), info[k][8])
        copies[k][8].start()
    for k in range(4):
        for n in (6, 7, 8):
            copies[k][n].wait_recv()

    def finish(b, total):
        gradient = tiles[b].astype(F32)
        for k in range(4):
            gradient = gradient + got[info[k][9] + b].astype(F32)
        step_field = STEP_RATE * gradient
        skyb[b] = skyb[b] - step_field
        squares = (step_field * step_field).reshape(TS // 8, 8, TS).sum(0)
        return total + squares[:, :128] + squares[:, 128:]

    squares = lax.fori_loop(0, BANDS, finish, jnp.zeros((8, 128), F32))
    c = pltpu.make_async_copy(skyb, out, lsem.at[0])
    c.start()

    def exchange(slots, place, value, devices, send_sems, recv_sems):
        slots[place] = value
        shares = [
            pltpu.make_async_remote_copy(
                src_ref=slots.at[place],
                dst_ref=slots.at[place],
                send_sem=send_sems.at[k],
                recv_sem=recv_sems.at[k],
                device_id=device,
                device_id_type=MESH,
            )
            for k, device in enumerate(devices)
        ]
        for share in shares:
            share.start()
        for share in shares:
            share.wait()
        return jnp.sum(slots[...], 0)

    squares = exchange(held, patch, squares, peers, tsem, tsem2)
    squares = exchange(held2, exp, squares, peers2, tsem3, tsem4)
    mean = jnp.sum(jnp.sum(squares, 0, keepdims=True), 1, keepdims=True) / (128 * BANDS * TS * TS)
    rms[...] = jnp.broadcast_to(jnp.sqrt(mean + 1e-06), rms.shape)
    for k in range(4):
        for c2 in copies[k]:
            c2.wait_send()
    c.wait()


def step(patch, band, gain, weight, taps, sky, pix):
    anys = pl.BlockSpec(memory_space=pl.ANY)
    vmem = pl.BlockSpec(memory_space=pltpu.VMEM)
    return pl.pallas_call(
        main_kernel,
        out_shape=(
            jax.ShapeDtypeStruct((BANDS, TS, TS), F32),
            jax.ShapeDtypeStruct((1, 128), F32),
        ),
        in_specs=[vmem] * 5 + [anys, anys],
        out_specs=(anys, vmem),
        scratch_shapes=[
            pltpu.VMEM((TILES, TS, TS), BF16),
            pltpu.VMEM((TILES, TS, TS), BF16),
            pltpu.VMEM((STAMPS, TS, TS), BF16),
            pltpu.VMEM((STAMPS, TS, TS), BF16),
            pltpu.VMEM((TS, TS), F32),
            pltpu.VMEM((PER, 4, TS, TS), BF16),
            pltpu.VMEM((PER, TS, TS), BF16),
            pltpu.VMEM((PER, TS, TS), BF16),
            pltpu.VMEM((BANDS, TS, TS), F32),
            pltpu.VMEM((4, 128, 128), F32),
            pltpu.VMEM((8, 128), jnp.int32),
            pltpu.VMEM((8, 128), F32),
            pltpu.SMEM((8, 128), jnp.int32),
            pltpu.SMEM((8, 128), F32),
            pltpu.VMEM((16, 8, 128), F32),
            pltpu.VMEM((8, 8, 128), F32),
            pltpu.SemaphoreType.DMA((4,)),
            pltpu.SemaphoreType.DMA((4, 8)),
            pltpu.SemaphoreType.DMA((4, 8)),
            pltpu.SemaphoreType.DMA((4, 9)),
            pltpu.SemaphoreType.DMA((4, 9)),
            pltpu.SemaphoreType.DMA((15,)),
            pltpu.SemaphoreType.DMA((15,)),
            pltpu.SemaphoreType.DMA((7,)),
            pltpu.SemaphoreType.DMA((7,)),
            pltpu.SemaphoreType.REGULAR,
            pltpu.SemaphoreType.REGULAR,
        ],
        compiler_params=pltpu.CompilerParams(
            collective_id=1, has_side_effects=True, vmem_limit_bytes=63 * 2**20 + 2**19
        ),
        name="step",
    )(patch, band, gain, weight, taps, sky, pix)


def per_device(
    sky_model, stamp_pixels, stamp_patch, stamp_band, psf_taps, stamp_gain, stamp_weight
):
    sky = sky_model.reshape(BANDS, TS, TS)
    taps = psf_taps.transpose(2, 1, 0)
    patch, band, gain, weight = (
        v.reshape(1, STAMPS) for v in (stamp_patch, stamp_band, stamp_gain, stamp_weight)
    )
    new_model, rms = step(patch, band, gain, weight, taps, sky, stamp_pixels)
    return (new_model.reshape(sky_model.shape), rms[0, 0])


def solution(mesh):
    return jax.shard_map(
        per_device,
        mesh=mesh,
        in_specs=(
            P("patch", "exp", None, None, None),
            P(("patch", "exp"), None, None),
            P(("patch", "exp"), None),
            P(("patch", "exp")),
            P(("patch", "exp"), None, None),
            P(("patch", "exp")),
            P(("patch", "exp")),
        ),
        out_specs=(P("patch", "exp", None, None, None), P()),
        check_vma=False,
    )
```

```python
import functools

import jax
import jax.numpy as jnp
from jax import lax
from jax.experimental import pallas as pl
from jax.experimental.pallas import tpu as pltpu
from jax.sharding import PartitionSpec as P

TS = 256
BANDS = 6
HALF = 3
STAMPS = 128
STEP_RATE = 0.2
F32, BF16 = jnp.float32, jnp.bfloat16
MESH = pl.DeviceIdType.MESH

UNITS = [
    (0, 0), (0, 1), (0, -1), (1, 0), (-1, 0),
    (1, -1), (-1, 1), (0, 2), (2, 0), (1, 1), (-1, -1),
    (2, 1), (1, 2), (2, -1), (-1, 2), (2, 2),
]
UNIT = {offset: number for number, offset in enumerate(UNITS)}
TILES = len(UNITS) * BANDS
LINKS = [(0, 1), (0, -1), (1, 0), (-1, 0)]
PER = 4


def place_on_torus():
    patch = lax.axis_index("patch")
    return patch // 4, lax.rem(patch, 4)


def neighbour(offset):
    z, x = place_on_torus()
    return lax.rem(z + offset[0] + 4, 4) * 4 + lax.rem(x + offset[1] + 4, 4)


def index_grids():
    return (
        lax.broadcasted_iota(jnp.int32, (128, 128), 0),
        lax.broadcasted_iota(jnp.int32, (128, 128), 1),
    )


def tap_rows(taps, rows):
    source, lane = index_grids()
    tap = jnp.where(lane <= 10, lane + 10, lane - 118)
    used = (lane <= 10) | (lane >= 118)
    rows[0] = jnp.zeros((128, 128), F32)
    for k in range(taps.shape[0]):
        rows[0, 2 * k : 2 * k + 2, :] = taps[k].astype(F32)
    lines = rows[0].T.astype(BF16)
    for m in range(4):
        wanted = 2 * (20 - tap if m % 2 else tap) + m // 2
        pick = jnp.where(used & (source == wanted), 1.0, 0.0).astype(BF16)
        rows[m] = dot(lines, pick)


def stamp_order(patch, band, gain, weight, ints, floats):
    z, x = place_on_torus()
    down, lane = index_grids()

    def across(line):
        return jnp.broadcast_to(line, (128, 128))

    def total(grid):
        return jnp.sum(grid, 0, keepdims=True)

    where = across(patch[...]).T
    dz = lax.rem(where // 4 - z + 4, 4)
    dx = lax.rem(lax.rem(where, 4) - x + 4, 4)
    offset = dz * 4 + dx
    unit = jnp.zeros_like(offset)
    for number, (a, b) in enumerate(UNITS):
        unit = jnp.where(offset == (a % 4) * 4 + b % 4, number, unit)
    tile_d = unit * BANDS + across(band[...]).T
    tile_l = tile_d.T
    rank_d, rank_l = tile_d * STAMPS + down, tile_l * STAMPS + lane
    before = rank_d < rank_l
    one, none = jnp.ones_like(down), jnp.zeros_like(down)
    spot = across(total(jnp.where(before, one, none))).T
    mates = across(total(jnp.where(before & (tile_d == tile_l), one, none))).T
    here = spot == lane
    ints[0:1, :] = total(jnp.where(here, down, none))
    ints[1:2, :] = total(jnp.where(here, tile_d, none))
    ints[2:3, :] = jnp.maximum(total(jnp.where(tile_d <= lane, one, none)) - 1, 0)
    zero = jnp.zeros((128, 128), F32)
    floats[0:1, :] = total(jnp.where(here & (mates > 0), zero + 1.0, zero))
    floats[1:2, :] = jnp.where(total(jnp.where(tile_d == lane, one, none)) > 0, 1.0, 0.0)
    floats[2:3, :] = total(jnp.where(here, across(gain[...].astype(F32)).T, zero))
    floats[3:4, :] = total(jnp.where(here, across(weight[...].astype(F32)).T, zero))


def build(row, dst):
    ring = pltpu.roll(jnp.broadcast_to(row, (128, 128)), 0, 1, stride=1, stride_axis=0)
    d = lax.broadcasted_iota(jnp.int32, (128, 128), 1) - lax.broadcasted_iota(
        jnp.int32, (128, 128), 0
    )
    zero = jnp.zeros_like(ring)
    diag = jnp.where(jnp.abs(d) < 64, ring, zero).astype(BF16)
    dst[0:128, 0:128] = diag
    dst[128:256, 128:256] = diag
    dst[112:128, 128:256] = jnp.where(d < -64, ring, zero)[112:].astype(BF16)
    dst[128:144, 0:128] = jnp.where(d > 64, ring, zero)[:16].astype(BF16)


def dot(a, b):
    return jnp.dot(a, b, preferred_element_type=F32)


def send(link, src, dst, send_sem, recv_sem):
    return pltpu.make_async_remote_copy(
        src_ref=src,
        dst_ref=dst,
        send_sem=send_sem,
        recv_sem=recv_sem,
        device_id={"patch": neighbour(LINKS[link])},
        device_id_type=MESH,
    )


def span(offset, half):
    first = UNIT[offset] * BANDS + half * HALF
    return slice(first, first + HALF)


def whole(offset):
    return slice(UNIT[offset] * BANDS, UNIT[offset] * BANDS + BANDS)


def seen_from(link, offset):
    dz, dx = ((a - b + 1) % 4 - 1 for a, b in zip(offset, link))
    return dz, dx


FAR = [
    [((1, -1), 1), ((2, 0), 0)],
    [((2, 0), 0), ((-1, 1), 1)],
    [((-1, 1), 1), ((0, 2), 0)],
    [((0, 2), 0), ((1, -1), 1)],
]


def gather_copies(got, ssem, rsem):
    table = []
    for k, link in enumerate(LINKS):
        dz, dx = link
        along_x, sign = dz == 0, dz + dx
        diag = [((s, 0), 1) if along_x else ((0, s), 0) for s in (sign, -sign)]
        straight = ((-dz, -dx), 0 if sign > 0 else 1)
        moves = [((0, 0), 0), ((0, 0), 1), diag[0], straight, diag[1], *FAR[k]]
        row = [
            send(k, got.at[span(a, h)], got.at[span(seen_from(link, a), h)], ssem.at[k, n], rsem.at[k, n])
            for n, (a, h) in enumerate(moves)
        ]
        rows = slice(k * 64, k * 64 + 64)
        via = (2, -dx) if along_x else (-dz, 2)
        row.append(
            send(k, got.at[whole(via), rows], got.at[whole((2, 2)), rows], ssem.at[k, 7], rsem.at[k, 7])
        )
        table.append(row)
    return table


def reduce_copies(tiles, got, ssem, rsem):
    copies, info = [], []
    for k, link in enumerate(LINKS):
        dz, dx = link
        late = 0 if dz + dx > 0 else 1
        early = 1 - late
        along_x = dz == 0
        far = (2, dx) if along_x else (dz, 2)
        straight = (0, 2) if along_x else (2, 0)
        sides = [(s, dx) if along_x else (dz, s) for s in (-dz - dx, dz + dx)]
        diag_half = 1 if along_x else 0
        rows_k = slice(k * 64, k * 64 + 64)
        diag, three, two, one = 6 + 6 * k, 30 + 6 * k, 54 + 3 * k, 66 + 6 * k
        row = [send(k, tiles.at[whole((2, 2)), rows_k], got.at[0:6, rows_k], ssem.at[k, 0], rsem.at[k, 0])]
        for n, (offset, h, dst) in enumerate(
            [
                (sides[0], diag_half, diag),
                (far, 0, three),
                (far, 1, three + 3),
                (sides[1], diag_half, diag + 3),
                (straight, late, two),
            ],
            1,
        ):
            row.append(send(k, tiles.at[span(offset, h)], got.at[dst : dst + 3], ssem.at[k, n], rsem.at[k, n]))
        for n, (tile, dst, count) in enumerate(
            [
                (span(link, early).start, one + early * 3, 2),
                (span(link, early).start + 2, one + early * 3 + 2, 1),
                (span(link, late).start, one + late * 3, 3),
            ],
            6,
        ):
            row.append(send(k, tiles.at[tile : tile + count], got.at[dst : dst + count], ssem.at[k, n], rsem.at[k, n]))
        copies.append(row)
        info.append((far, straight, sides, diag_half, early, late, diag, three, two, one))

    return copies, info


def main_kernel(patch_of, band_of, gain_of, weight_of, taps, sky, pix, out, rms,
                got, tiles, pixv, seg, carry, mats, blur, resi, skyb, rows, intv, floatv, ints, floats, held, held2,
                lsem, ssem, rsem, ssem2, rsem2, tsem, tsem2, tsem3, tsem4, early, free):
    sky_load = pltpu.make_async_copy(sky, skyb, lsem.at[0])
    sky_load.start()
    patch, exp = lax.axis_index("patch"), lax.axis_index("exp")
    peers = [{"patch": lax.rem(patch + k, 16)} for k in range(1, 16)]
    peers2 = [{"exp": lax.rem(exp + k, 8)} for k in range(1, 8)]
    barrier = pltpu.get_barrier_semaphore()
    greeted = [{"patch": neighbour(link)} for link in LINKS] + peers2
    for peer in greeted:
        pl.semaphore_signal(barrier, inc=1, device_id=peer, device_id_type=MESH)
    pix_load = pltpu.make_async_copy(pix, pixv, lsem.at[1])
    sky_load.wait()

    @pl.loop(0, BANDS)
    def _(b):
        half = skyb[b].astype(BF16)
        got[b] = half
        tiles[b] = half

    pl.semaphore_wait(barrier, len(greeted))
    moves = gather_copies(got, ssem, rsem)
    for k, link in enumerate(LINKS):
        for n in (0, 1) if link[0] == 0 else (1, 0):
            moves[k][n].start()
    stamp_order(patch_of, band_of, gain_of, weight_of, intv, floatv)
    tables = [
        pltpu.make_async_copy(intv, ints, lsem.at[2]),
        pltpu.make_async_copy(floatv, floats, lsem.at[3]),
    ]
    for c in tables:
        c.start()
    tap_rows(taps, rows)
    pix_load.start()
    carry[...] = jnp.zeros_like(carry)
    mats[...] = jnp.zeros_like(mats)

    def keep(*offsets):
        for offset in offsets:

            @pl.loop(UNIT[offset] * BANDS, UNIT[offset] * BANDS + BANDS)
            def _(t):
                tiles[t] = got[t]

    def body(step, nothing):
        at = [step * PER + u for u in range(PER)]
        idx = [ints[0, a] for a in at]
        for u in range(PER):
            for m in range(4):
                build(rows[m, pl.ds(idx[u], 1), :], mats.at[u, m])
        g = [floats[2, a] for a in at]
        w = [floats[3, a] for a in at]
        for u in range(PER):
            blur[u] = dot(tiles[ints[1, at[u]]], mats[u, 3]).astype(BF16)
        for u in range(PER):
            predicted = g[u] * dot(mats[u, 0], blur[u])
            resi[u] = (w[u] * (predicted - pixv[idx[u]].astype(F32))).astype(BF16)
        for u in range(PER):
            blur[u] = dot(mats[u, 1], resi[u]).astype(BF16)
        for u in range(PER):
            total = carry[...] * floats[0, at[u]] + g[u] * dot(blur[u], mats[u, 2])
            carry[...] = total
            seg[at[u]] = total.astype(BF16)
        return nothing

    def stamps(lo, hi):
        lax.fori_loop(lo // PER, hi // PER, body, 0)

    def collect(lo, hi):
        @pl.loop(lo * BANDS, hi * BANDS)
        def _(t):
            tiles[t] = (seg[ints[2, t]].astype(F32) * floats[1, t]).astype(BF16)

    def tell(semaphore):
        for link in LINKS:
            pl.semaphore_signal(
                semaphore, inc=1, device_id={"patch": neighbour(link)}, device_id_type=MESH
            )

    copies, info = reduce_copies(tiles, got, ssem2, rsem2)

    def arrive(*numbers):
        for k in range(4):
            for n in numbers:
                moves[k][n].wait_recv()

    def forward(*numbers):
        for k in range(4):
            for n in numbers:
                moves[k][n].start()

    def gone(*numbers):
        for k in range(4):
            for n in numbers:
                moves[k][n].wait_send()

    for k, link in enumerate(LINKS):
        moves[k][0 if link[0] == 0 else 1].wait_recv()
    forward(2)
    for k, link in enumerate(LINKS):
        moves[k][1 if link[0] == 0 else 0].wait_recv()
    forward(3, 4)
    keep(*UNITS[1:5])
    for c in tables:
        c.wait()
    pix_load.wait()
    arrive(2)
    keep(*UNITS[5:7])
    stamps(0, 20)
    arrive(3)
    forward(5, 6)
    keep(*UNITS[7:9])
    stamps(20, 44)
    arrive(4)
    keep(*UNITS[9:11])
    stamps(44, 68)
    arrive(5)
    for k in (1, 3):
        moves[k][7].start()
    keep(*UNITS[11:13])
    gone(2, 3, 4)
    tell(early)
    stamps(68, 92)
    arrive(6)
    for k in (0, 2):
        moves[k][7].start()
    keep(*UNITS[13:15])
    collect(5, 7)
    pl.semaphore_wait(early, 4)
    for k in range(4):
        copies[k][1].start()
    stamps(92, 116)
    arrive(7)
    keep(*UNITS[15:16])
    gone(0, 1, 5, 6, 7)
    tell(free)
    stamps(116, 128)

    def add_into(slots, src):
        @pl.loop(0, HALF)
        def _(t):
            d = slots.start + t
            tiles[d] = (tiles[d].astype(F32) + got[src + t].astype(F32)).astype(BF16)

    collect(15, 16)
    pl.semaphore_wait(free, 4)
    for k in range(4):
        copies[k][0].start()
    collect(9, 11)
    for k in range(4):
        copies[k][4].start()
    collect(11, 15)
    for k in range(4):
        copies[k][0].wait_recv()
        first = UNIT[info[k][0]] * BANDS

        @pl.loop(0, BANDS)
        def _(b):
            r = slice(k * 64, k * 64 + 64)
            tiles[first + b, r] = (tiles[first + b, r].astype(F32) + got[b, r].astype(F32)).astype(BF16)

        for n in (2, 3):
            copies[k][n].start()
    collect(0, 5)
    collect(7, 9)
    for n in (1, 4):
        for k in range(4):
            sides, diag_half = info[k][2:4]
            copies[k][n].wait_recv()
            dz, dx = sides[n // 4]
            target = (dz, 0) if LINKS[k][0] == 0 else (0, dx)
            add_into(span(target, diag_half), info[k][6] + n // 4 * HALF)
    for k in range(4):
        copies[k][6].start()
    for h in range(2):
        for k in range(4):
            copies[k][2 + h].wait_recv()
            target = (2, 0) if LINKS[k][0] == 0 else (0, 2)
            add_into(span(target, h), info[k][7] + h * HALF)
        for k in range(4):
            if info[k][5] == h:
                copies[k][5].start()
                copies[k][7].start()
    for k in range(4):
        copies[k][5].wait_recv()
        add_into(span(LINKS[k], info[k][5]), info[k][8])
        copies[k][8].start()
    for k in range(4):
        for n in (6, 7, 8):
            copies[k][n].wait_recv()

    def finish(b, total):
        gradient = tiles[b].astype(F32)
        for k in range(4):
            gradient = gradient + got[info[k][9] + b].astype(F32)
        step_field = STEP_RATE * gradient
        skyb[b] = skyb[b] - step_field
        squares = (step_field * step_field).reshape(TS // 8, 8, TS).sum(0)
        return total + squares[:, :128] + squares[:, 128:]

    squares = lax.fori_loop(0, BANDS, finish, jnp.zeros((8, 128), F32))
    c = pltpu.make_async_copy(skyb, out, lsem.at[0])
    c.start()

    def exchange(slots, place, value, devices, send_sems, recv_sems):
        slots[place] = value
        shares = [
            pltpu.make_async_remote_copy(
                src_ref=slots.at[place],
                dst_ref=slots.at[place],
                send_sem=send_sems.at[k],
                recv_sem=recv_sems.at[k],
                device_id=device,
                device_id_type=MESH,
            )
            for k, device in enumerate(devices)
        ]
        for share in shares:
            share.start()
        for share in shares:
            share.wait()
        return jnp.sum(slots[...], 0)

    squares = exchange(held, patch, squares, peers, tsem, tsem2)
    squares = exchange(held2, exp, squares, peers2, tsem3, tsem4)
    mean = jnp.sum(jnp.sum(squares, 0, keepdims=True), 1, keepdims=True) / (128 * BANDS * TS * TS)
    rms[...] = jnp.broadcast_to(jnp.sqrt(mean + 1e-06), rms.shape)
    for k in range(4):
        for c2 in copies[k]:
            c2.wait_send()
    c.wait()


def step(patch, band, gain, weight, taps, sky, pix):
    anys = pl.BlockSpec(memory_space=pl.ANY)
    vmem = pl.BlockSpec(memory_space=pltpu.VMEM)
    return pl.pallas_call(
        main_kernel,
        out_shape=(
            jax.ShapeDtypeStruct((BANDS, TS, TS), F32),
            jax.ShapeDtypeStruct((1, 128), F32),
        ),
        in_specs=[vmem] * 5 + [anys, anys],
        out_specs=(anys, vmem),
        scratch_shapes=[
            pltpu.VMEM((TILES, TS, TS), BF16),
            pltpu.VMEM((TILES, TS, TS), BF16),
            pltpu.VMEM((STAMPS, TS, TS), BF16),
            pltpu.VMEM((STAMPS, TS, TS), BF16),
            pltpu.VMEM((TS, TS), F32),
            pltpu.VMEM((PER, 4, TS, TS), BF16),
            pltpu.VMEM((PER, TS, TS), BF16),
            pltpu.VMEM((PER, TS, TS), BF16),
            pltpu.VMEM((BANDS, TS, TS), F32),
            pltpu.VMEM((4, 128, 128), F32),
            pltpu.VMEM((8, 128), jnp.int32),
            pltpu.VMEM((8, 128), F32),
            pltpu.SMEM((8, 128), jnp.int32),
            pltpu.SMEM((8, 128), F32),
            pltpu.VMEM((16, 8, 128), F32),
            pltpu.VMEM((8, 8, 128), F32),
            pltpu.SemaphoreType.DMA((4,)),
            pltpu.SemaphoreType.DMA((4, 8)),
            pltpu.SemaphoreType.DMA((4, 8)),
            pltpu.SemaphoreType.DMA((4, 9)),
            pltpu.SemaphoreType.DMA((4, 9)),
            pltpu.SemaphoreType.DMA((15,)),
            pltpu.SemaphoreType.DMA((15,)),
            pltpu.SemaphoreType.DMA((7,)),
            pltpu.SemaphoreType.DMA((7,)),
            pltpu.SemaphoreType.REGULAR,
            pltpu.SemaphoreType.REGULAR,
        ],
        compiler_params=pltpu.CompilerParams(
            collective_id=1, has_side_effects=True, vmem_limit_bytes=63 * 2**20 + 2**19
        ),
        name="step",
    )(patch, band, gain, weight, taps, sky, pix)


def per_device(
    sky_model, stamp_pixels, stamp_patch, stamp_band, psf_taps, stamp_gain, stamp_weight
):
    sky = sky_model.reshape(BANDS, TS, TS)
    taps = psf_taps.transpose(2, 1, 0)
    patch, band, gain, weight = (
        v.reshape(1, STAMPS) for v in (stamp_patch, stamp_band, stamp_gain, stamp_weight)
    )
    new_model, rms = step(patch, band, gain, weight, taps, sky, stamp_pixels)
    return (new_model.reshape(sky_model.shape), rms[0, 0])


def solution(mesh):
    return jax.shard_map(
        per_device,
        mesh=mesh,
        in_specs=(
            P("patch", "exp", None, None, None),
            P(("patch", "exp"), None, None),
            P(("patch", "exp"), None),
            P(("patch", "exp")),
            P(("patch", "exp"), None, None),
            P(("patch", "exp")),
            P(("patch", "exp")),
        ),
        out_specs=(P("patch", "exp", None, None, None), P()),
        check_vma=False,
    )
```

```python
import functools

import jax
import jax.numpy as jnp
from jax import lax
from jax.experimental import pallas as pl
from jax.experimental.pallas import tpu as pltpu
from jax.sharding import PartitionSpec as P

TS = 256
BANDS = 6
HALF = 3
STAMPS = 128
STEP_RATE = 0.2
F32, BF16 = jnp.float32, jnp.bfloat16
MESH = pl.DeviceIdType.MESH

UNITS = [
    (0, 0), (0, 1), (0, -1), (1, 0), (-1, 0),
    (1, -1), (-1, 1), (0, 2), (2, 0), (1, 1), (-1, -1),
    (2, 1), (1, 2), (2, -1), (-1, 2), (2, 2),
]
UNIT = {offset: number for number, offset in enumerate(UNITS)}
TILES = len(UNITS) * BANDS
LINKS = [(0, 1), (0, -1), (1, 0), (-1, 0)]
PER = 4


def place_on_torus():
    patch = lax.axis_index("patch")
    return patch // 4, lax.rem(patch, 4)


def neighbour(offset):
    z, x = place_on_torus()
    return lax.rem(z + offset[0] + 4, 4) * 4 + lax.rem(x + offset[1] + 4, 4)


def index_grids():
    return (
        lax.broadcasted_iota(jnp.int32, (128, 128), 0),
        lax.broadcasted_iota(jnp.int32, (128, 128), 1),
    )


def tap_rows(taps, rows):
    source, lane = index_grids()
    tap = jnp.where(lane <= 10, lane + 10, lane - 118)
    used = (lane <= 10) | (lane >= 118)
    rows[0] = jnp.zeros((128, 128), F32)
    for k in range(taps.shape[0]):
        rows[0, 2 * k : 2 * k + 2, :] = taps[k].astype(F32)
    lines = rows[0].T.astype(BF16)
    for m in range(4):
        wanted = 2 * (20 - tap if m % 2 else tap) + m // 2
        pick = jnp.where(used & (source == wanted), 1.0, 0.0).astype(BF16)
        rows[m] = dot(lines, pick)


def stamp_order(patch, band, gain, weight, ints, floats):
    z, x = place_on_torus()
    down, lane = index_grids()

    def across(line):
        return jnp.broadcast_to(line, (128, 128))

    def total(grid):
        return jnp.sum(grid, 0, keepdims=True)

    where = across(patch[...]).T
    dz = lax.rem(where // 4 - z + 4, 4)
    dx = lax.rem(lax.rem(where, 4) - x + 4, 4)
    offset = dz * 4 + dx
    unit = jnp.zeros_like(offset)
    for number, (a, b) in enumerate(UNITS):
        unit = jnp.where(offset == (a % 4) * 4 + b % 4, number, unit)
    tile_d = unit * BANDS + across(band[...]).T
    tile_l = tile_d.T
    rank_d, rank_l = tile_d * STAMPS + down, tile_l * STAMPS + lane
    before = rank_d < rank_l
    one, none = jnp.ones_like(down), jnp.zeros_like(down)
    spot = across(total(jnp.where(before, one, none))).T
    mates = across(total(jnp.where(before & (tile_d == tile_l), one, none))).T
    here = spot == lane
    ints[0:1, :] = total(jnp.where(here, down, none))
    ints[1:2, :] = total(jnp.where(here, tile_d, none))
    ints[2:3, :] = jnp.maximum(total(jnp.where(tile_d <= lane, one, none)) - 1, 0)
    zero = jnp.zeros((128, 128), F32)
    floats[0:1, :] = total(jnp.where(here & (mates > 0), zero + 1.0, zero))
    floats[1:2, :] = jnp.where(total(jnp.where(tile_d == lane, one, none)) > 0, 1.0, 0.0)
    floats[2:3, :] = total(jnp.where(here, across(gain[...].astype(F32)).T, zero))
    floats[3:4, :] = total(jnp.where(here, across(weight[...].astype(F32)).T, zero))


def build(row, dst):
    ring = pltpu.roll(jnp.broadcast_to(row, (128, 128)), 0, 1, stride=1, stride_axis=0)
    d = lax.broadcasted_iota(jnp.int32, (128, 128), 1) - lax.broadcasted_iota(
        jnp.int32, (128, 128), 0
    )
    zero = jnp.zeros_like(ring)
    diag = jnp.where(jnp.abs(d) < 64, ring, zero).astype(BF16)
    dst[0:128, 0:128] = diag
    dst[128:256, 128:256] = diag
    dst[112:128, 128:256] = jnp.where(d < -64, ring, zero)[112:].astype(BF16)
    dst[128:144, 0:128] = jnp.where(d > 64, ring, zero)[:16].astype(BF16)


def dot(a, b):
    return jnp.dot(a, b, preferred_element_type=F32)


def send(link, src, dst, send_sem, recv_sem):
    return pltpu.make_async_remote_copy(
        src_ref=src,
        dst_ref=dst,
        send_sem=send_sem,
        recv_sem=recv_sem,
        device_id={"patch": neighbour(LINKS[link])},
        device_id_type=MESH,
    )


def span(offset, half):
    first = UNIT[offset] * BANDS + half * HALF
    return slice(first, first + HALF)


def whole(offset):
    return slice(UNIT[offset] * BANDS, UNIT[offset] * BANDS + BANDS)


def seen_from(link, offset):
    dz, dx = ((a - b + 1) % 4 - 1 for a, b in zip(offset, link))
    return dz, dx


FAR = [
    [((1, -1), 1), ((2, 0), 0)],
    [((2, 0), 0), ((-1, 1), 1)],
    [((-1, 1), 1), ((0, 2), 0)],
    [((0, 2), 0), ((1, -1), 1)],
]


def gather_copies(got, ssem, rsem):
    table = []
    for k, link in enumerate(LINKS):
        dz, dx = link
        along_x, sign = dz == 0, dz + dx
        diag = [((s, 0), 1) if along_x else ((0, s), 0) for s in (sign, -sign)]
        straight = ((-dz, -dx), 0 if sign > 0 else 1)
        moves = [((0, 0), 0), ((0, 0), 1), diag[0], straight, diag[1], *FAR[k]]
        row = [
            send(k, got.at[span(a, h)], got.at[span(seen_from(link, a), h)], ssem.at[k, n], rsem.at[k, n])
            for n, (a, h) in enumerate(moves)
        ]
        rows = slice(k * 64, k * 64 + 64)
        via = (2, -dx) if along_x else (-dz, 2)
        row.append(
            send(k, got.at[whole(via), rows], got.at[whole((2, 2)), rows], ssem.at[k, 7], rsem.at[k, 7])
        )
        table.append(row)
    return table


def reduce_copies(tiles, got, ssem, rsem):
    copies, info = [], []
    for k, link in enumerate(LINKS):
        dz, dx = link
        late = 0 if dz + dx > 0 else 1
        early = 1 - late
        along_x = dz == 0
        far = (2, dx) if along_x else (dz, 2)
        straight = (0, 2) if along_x else (2, 0)
        sides = [(s, dx) if along_x else (dz, s) for s in (-dz - dx, dz + dx)]
        diag_half = 1 if along_x else 0
        rows_k = slice(k * 64, k * 64 + 64)
        diag, three, two, one = 6 + 6 * k, 30 + 6 * k, 54 + 3 * k, 66 + 6 * k
        row = [send(k, tiles.at[whole((2, 2)), rows_k], got.at[0:6, rows_k], ssem.at[k, 0], rsem.at[k, 0])]
        for n, (offset, h, dst) in enumerate(
            [
                (sides[0], diag_half, diag),
                (far, 0, three),
                (far, 1, three + 3),
                (sides[1], diag_half, diag + 3),
                (straight, late, two),
            ],
            1,
        ):
            row.append(send(k, tiles.at[span(offset, h)], got.at[dst : dst + 3], ssem.at[k, n], rsem.at[k, n]))
        for n, (tile, dst, count) in enumerate(
            [
                (span(link, early).start, one + early * 3, 2),
                (span(link, early).start + 2, one + early * 3 + 2, 1),
                (span(link, late).start, one + late * 3, 3),
            ],
            6,
        ):
            row.append(send(k, tiles.at[tile : tile + count], got.at[dst : dst + count], ssem.at[k, n], rsem.at[k, n]))
        copies.append(row)
        info.append((far, straight, sides, diag_half, early, late, diag, three, two, one))

    return copies, info


def main_kernel(patch_of, band_of, gain_of, weight_of, taps, sky, pix, out, rms,
                got, tiles, pixv, seg, carry, mats, blur, resi, skyb, rows, intv, floatv, ints, floats, held, held2,
                lsem, ssem, rsem, ssem2, rsem2, tsem, tsem2, tsem3, tsem4, early, free):
    sky_load = pltpu.make_async_copy(sky, skyb, lsem.at[0])
    sky_load.start()
    patch, exp = lax.axis_index("patch"), lax.axis_index("exp")
    peers = [{"patch": lax.rem(patch + k, 16)} for k in range(1, 16)]
    peers2 = [{"exp": lax.rem(exp + k, 8)} for k in range(1, 8)]
    barrier = pltpu.get_barrier_semaphore()
    greeted = [{"patch": neighbour(link)} for link in LINKS] + peers2
    for peer in greeted:
        pl.semaphore_signal(barrier, inc=1, device_id=peer, device_id_type=MESH)
    pix_load = pltpu.make_async_copy(pix, pixv, lsem.at[1])
    sky_load.wait()

    @pl.loop(0, BANDS)
    def _(b):
        half = skyb[b].astype(BF16)
        got[b] = half
        tiles[b] = half

    pl.semaphore_wait(barrier, len(greeted))
    moves = gather_copies(got, ssem, rsem)
    for k, link in enumerate(LINKS):
        for n in (0, 1) if link[0] == 0 else (1, 0):
            moves[k][n].start()
    stamp_order(patch_of, band_of, gain_of, weight_of, intv, floatv)
    tables = [
        pltpu.make_async_copy(intv, ints, lsem.at[2]),
        pltpu.make_async_copy(floatv, floats, lsem.at[3]),
    ]
    for c in tables:
        c.start()
    tap_rows(taps, rows)
    pix_load.start()
    carry[...] = jnp.zeros_like(carry)
    mats[...] = jnp.zeros_like(mats)

    def keep(*offsets):
        for offset in offsets:

            @pl.loop(UNIT[offset] * BANDS, UNIT[offset] * BANDS + BANDS)
            def _(t):
                tiles[t] = got[t]

    def body(step, nothing):
        at = [step * PER + u for u in range(PER)]
        idx = [ints[0, a] for a in at]
        for u in range(PER):
            for m in range(4):
                build(rows[m, pl.ds(idx[u], 1), :], mats.at[u, m])
        g = [floats[2, a] for a in at]
        w = [floats[3, a] for a in at]
        for u in range(PER):
            blur[u] = dot(tiles[ints[1, at[u]]], mats[u, 3]).astype(BF16)
        for u in range(PER):
            predicted = g[u] * dot(mats[u, 0], blur[u])
            resi[u] = (w[u] * (predicted - pixv[idx[u]].astype(F32))).astype(BF16)
        for u in range(PER):
            blur[u] = dot(mats[u, 1], resi[u]).astype(BF16)
        for u in range(PER):
            total = carry[...] * floats[0, at[u]] + g[u] * dot(blur[u], mats[u, 2])
            carry[...] = total
            seg[at[u]] = total.astype(BF16)
        return nothing

    def stamps(lo, hi):
        lax.fori_loop(lo // PER, hi // PER, body, 0)

    def collect(lo, hi):
        @pl.loop(lo * BANDS, hi * BANDS)
        def _(t):
            tiles[t] = (seg[ints[2, t]].astype(F32) * floats[1, t]).astype(BF16)

    def tell(semaphore):
        for link in LINKS:
            pl.semaphore_signal(
                semaphore, inc=1, device_id={"patch": neighbour(link)}, device_id_type=MESH
            )

    copies, info = reduce_copies(tiles, got, ssem2, rsem2)

    def arrive(*numbers):
        for k in range(4):
            for n in numbers:
                moves[k][n].wait_recv()

    def forward(*numbers):
        for k in range(4):
            for n in numbers:
                moves[k][n].start()

    def gone(*numbers):
        for k in range(4):
            for n in numbers:
                moves[k][n].wait_send()

    for k, link in enumerate(LINKS):
        moves[k][0 if link[0] == 0 else 1].wait_recv()
    forward(2)
    for k, link in enumerate(LINKS):
        moves[k][1 if link[0] == 0 else 0].wait_recv()
    forward(3, 4)
    keep(*UNITS[1:5])
    for c in tables:
        c.wait()
    pix_load.wait()
    arrive(2)
    keep(*UNITS[5:7])
    stamps(0, 20)
    arrive(3)
    forward(5, 6)
    keep(*UNITS[7:9])
    stamps(20, 44)
    arrive(4)
    keep(*UNITS[9:11])
    stamps(44, 68)
    arrive(5)
    for k in (1, 3):
        moves[k][7].start()
    keep(*UNITS[11:13])
    gone(2, 3, 4)
    tell(early)
    stamps(68, 92)
    arrive(6)
    for k in (0, 2):
        moves[k][7].start()
    keep(*UNITS[13:15])
    collect(5, 7)
    pl.semaphore_wait(early, 4)
    for k in range(4):
        copies[k][1].start()
    stamps(92, 116)
    arrive(7)
    keep(*UNITS[15:16])
    gone(0, 1, 5, 6, 7)
    tell(free)
    stamps(116, 128)

    def add_into(slots, src):
        @pl.loop(0, HALF)
        def _(t):
            d = slots.start + t
            tiles[d] = (tiles[d].astype(F32) + got[src + t].astype(F32)).astype(BF16)

    collect(15, 16)
    pl.semaphore_wait(free, 4)
    for k in range(4):
        copies[k][0].start()
    collect(9, 11)
    for k in range(4):
        copies[k][4].start()
    collect(11, 15)
    for k in range(4):
        copies[k][0].wait_recv()
        first = UNIT[info[k][0]] * BANDS

        @pl.loop(0, BANDS)
        def _(b):
            r = slice(k * 64, k * 64 + 64)
            tiles[first + b, r] = (tiles[first + b, r].astype(F32) + got[b, r].astype(F32)).astype(BF16)

        for n in (2, 3):
            copies[k][n].start()
    collect(0, 5)
    collect(7, 9)
    for n in (1, 4):
        for k in range(4):
            sides, diag_half = info[k][2:4]
            copies[k][n].wait_recv()
            dz, dx = sides[n // 4]
            target = (dz, 0) if LINKS[k][0] == 0 else (0, dx)
            add_into(span(target, diag_half), info[k][6] + n // 4 * HALF)
    for k in range(4):
        copies[k][6].start()
    for h in range(2):
        for k in range(4):
            copies[k][2 + h].wait_recv()
            target = (2, 0) if LINKS[k][0] == 0 else (0, 2)
            add_into(span(target, h), info[k][7] + h * HALF)
        for k in range(4):
            if info[k][5] == h:
                copies[k][5].start()
                copies[k][7].start()
    for k in range(4):
        copies[k][5].wait_recv()
        add_into(span(LINKS[k], info[k][5]), info[k][8])
        copies[k][8].start()
    for k in range(4):
        for n in (6, 7, 8):
            copies[k][n].wait_recv()

    def step_of(b):
        gradient = tiles[b].astype(F32)
        for k in range(4):
            gradient = gradient + got[info[k][9] + b].astype(F32)
        return STEP_RATE * gradient

    def square(b, total):
        step_field = step_of(b)
        squares = (step_field * step_field).reshape(TS // 8, 8, TS).sum(0)
        return total + squares[:, :128] + squares[:, 128:]

    def exchange(slots, place, value, devices, send_sems, recv_sems):
        slots[place] = value
        shares = [
            pltpu.make_async_remote_copy(
                src_ref=slots.at[place],
                dst_ref=slots.at[place],
                send_sem=send_sems.at[k],
                recv_sem=recv_sems.at[k],
                device_id=device,
                device_id_type=MESH,
            )
            for k, device in enumerate(devices)
        ]
        for share in shares:
            share.start()
        return shares

    squares = lax.fori_loop(0, BANDS, square, jnp.zeros((8, 128), F32))
    shares = exchange(held, patch, squares, peers, tsem, tsem2)

    @pl.loop(0, BANDS)
    def _(b):
        skyb[b] = skyb[b] - step_of(b)

    c = pltpu.make_async_copy(skyb, out, lsem.at[0])
    c.start()
    for share in shares:
        share.wait_recv()
    shares2 = exchange(held2, exp, jnp.sum(held[...], 0), peers2, tsem3, tsem4)
    for share in shares:
        share.wait_send()
    for k in range(4):
        for c2 in copies[k]:
            c2.wait_send()
    for share in shares2:
        share.wait_recv()
    squares = jnp.sum(held2[...], 0)
    mean = jnp.sum(jnp.sum(squares, 0, keepdims=True), 1, keepdims=True) / (128 * BANDS * TS * TS)
    rms[...] = jnp.broadcast_to(jnp.sqrt(mean + 1e-06), rms.shape)
    for share in shares2:
        share.wait_send()
    c.wait()


def step(patch, band, gain, weight, taps, sky, pix):
    anys = pl.BlockSpec(memory_space=pl.ANY)
    vmem = pl.BlockSpec(memory_space=pltpu.VMEM)
    return pl.pallas_call(
        main_kernel,
        out_shape=(
            jax.ShapeDtypeStruct((BANDS, TS, TS), F32),
            jax.ShapeDtypeStruct((1, 128), F32),
        ),
        in_specs=[vmem] * 5 + [anys, anys],
        out_specs=(anys, vmem),
        scratch_shapes=[
            pltpu.VMEM((TILES, TS, TS), BF16),
            pltpu.VMEM((TILES, TS, TS), BF16),
            pltpu.VMEM((STAMPS, TS, TS), BF16),
            pltpu.VMEM((STAMPS, TS, TS), BF16),
            pltpu.VMEM((TS, TS), F32),
            pltpu.VMEM((PER, 4, TS, TS), BF16),
            pltpu.VMEM((PER, TS, TS), BF16),
            pltpu.VMEM((PER, TS, TS), BF16),
            pltpu.VMEM((BANDS, TS, TS), F32),
            pltpu.VMEM((4, 128, 128), F32),
            pltpu.VMEM((8, 128), jnp.int32),
            pltpu.VMEM((8, 128), F32),
            pltpu.SMEM((8, 128), jnp.int32),
            pltpu.SMEM((8, 128), F32),
            pltpu.VMEM((16, 8, 128), F32),
            pltpu.VMEM((8, 8, 128), F32),
            pltpu.SemaphoreType.DMA((4,)),
            pltpu.SemaphoreType.DMA((4, 8)),
            pltpu.SemaphoreType.DMA((4, 8)),
            pltpu.SemaphoreType.DMA((4, 9)),
            pltpu.SemaphoreType.DMA((4, 9)),
            pltpu.SemaphoreType.DMA((15,)),
            pltpu.SemaphoreType.DMA((15,)),
            pltpu.SemaphoreType.DMA((7,)),
            pltpu.SemaphoreType.DMA((7,)),
            pltpu.SemaphoreType.REGULAR,
            pltpu.SemaphoreType.REGULAR,
        ],
        compiler_params=pltpu.CompilerParams(
            collective_id=1, has_side_effects=True, vmem_limit_bytes=63 * 2**20 + 2**19
        ),
        name="step",
    )(patch, band, gain, weight, taps, sky, pix)


def per_device(
    sky_model, stamp_pixels, stamp_patch, stamp_band, psf_taps, stamp_gain, stamp_weight
):
    sky = sky_model.reshape(BANDS, TS, TS)
    taps = psf_taps.transpose(2, 1, 0)
    patch, band, gain, weight = (
        v.reshape(1, STAMPS) for v in (stamp_patch, stamp_band, stamp_gain, stamp_weight)
    )
    new_model, rms = step(patch, band, gain, weight, taps, sky, stamp_pixels)
    return (new_model.reshape(sky_model.shape), rms[0, 0])


def solution(mesh):
    return jax.shard_map(
        per_device,
        mesh=mesh,
        in_specs=(
            P("patch", "exp", None, None, None),
            P(("patch", "exp"), None, None),
            P(("patch", "exp"), None),
            P(("patch", "exp")),
            P(("patch", "exp"), None, None),
            P(("patch", "exp")),
            P(("patch", "exp")),
        ),
        out_specs=(P("patch", "exp", None, None, None), P()),
        check_vma=False,
    )
```
